32 devices in a mesh: seq: 16 (over z, y, x), head: 2 (over core).
Axes of the slice: x: 2, y: 2, z: 4, core: 2. Of those that a mesh axis runs over, the one named last changes fastest.
Arguments:
- queries: bfloat16 [12288, 1024], P('seq', 'head'), may hold values from -12 to 12
- keys: bfloat16 [12288, 1024], P('seq', 'head'), may hold values from -6 to 6
- values: bfloat16 [12288, 1024], P('seq', 'head'), may hold values from -6 to 6
- rates: float32 [12288, 2], P('seq', 'head'), may hold values from 0.02 to 1
- w_gate: bfloat16 [1024, 512], P('head'), may hold values from -0.25 to 0.25
- w_up: bfloat16 [1024, 512], P('head'), may hold values from -0.25 to 0.25
- w_down: bfloat16 [1024, 512], P('head'), may hold values from -0.25 to 0.25
- out_gain: float32 [1024], P('head'), may hold values from 0.1 to 1.9
Outputs:
- output: bfloat16 [12288, 1024], P('seq', 'head')
- next_gate: bfloat16 [1024, 512], P(('head', 'seq'))
- next_up: bfloat16 [1024, 512], P(('head', 'seq'))
- next_down: bfloat16 [1024, 512], P(('head', 'seq'))
The draws below stay inside these ranges and needn't reach their ends.
All inputs are finite; a program needn't handle non-finite values.
Results may differ from the reference program's by a relative error of at most 0.0077.
Values may be sent and summed in bfloat16 or wider, within the bound.
No kernel may reach another device: no remote copies, remote signals or barrier semaphores. Data moves between devices by JAX's collectives and lax.ppermute only.
A program may use at most 64 MiB of HBM per device.

```python
import math
import jax
import jax.numpy as jnp
from jax import lax

FW_DIM = 512
ATT_DIM = 128
HIDDEN_SIZE = 512
WINDOW = 512
TOK_DEV = 768
TOKENS = 12288
HEADS = 2
D = 1024
HID_ALL = 1024
N_SEQ = 16
N_HEAD = 2


def block_levels(key, extent, cuts, smallest, high):
    gain = 1.0
    for axis_at, parts in cuts:
        steps = jax.random.uniform(jax.random.fold_in(jax.random.fold_in(key, 6), axis_at), (parts,), jnp.float32, smallest / len(cuts), high / len(cuts))
        gain = gain * jnp.repeat(jnp.exp(steps), extent[axis_at] // parts).reshape((-1,) + (1,) * (len(extent) - 1 - axis_at))
    return gain


def noise(key, dims, spread, limit, cuts=(), held_as=jnp.bfloat16):
    entries = jax.random.normal(key, dims, jnp.float32) * spread
    if len(cuts) > 0:
        entries = block_levels(key, dims, cuts, -0.22, 0.18) * entries
    return jnp.clip(entries, min=-limit, max=limit).astype(held_as)


def setup_inputs(seed: int = 0) -> dict:
    streams_of = jax.random.split(jax.random.key(seed), 9)
    return {
        "queries": noise(streams_of[0], (TOKENS, D), 2.0, 12.0, ((0, 16), (1, 2))),
        "keys": noise(streams_of[1], (TOKENS, D), 1.0, 6.0, ((0, 16), (1, 2))),
        "values": noise(streams_of[2], (TOKENS, D), 1.0, 6.0, ((0, 16), (1, 2))),
        "rates": jnp.clip(jnp.exp(math.log(1.0) - 3.912023 * jax.random.uniform(streams_of[3], (TOKENS, HEADS), jnp.float32) ** block_levels(streams_of[3], (TOKENS, HEADS), ((0, 16), (1, 2)), -0.2, 0.2)), 0.02, 1.0),
        "w_gate": noise(streams_of[4], (D, HIDDEN_SIZE), FW_DIM ** -0.5, 0.25, ((0, 2),)),
        "w_up": noise(streams_of[5], (D, HIDDEN_SIZE), FW_DIM ** -0.5, 0.25, ((0, 2),)),
        "w_down": noise(streams_of[6], (HID_ALL, FW_DIM), HIDDEN_SIZE ** -0.5, 0.25, ((0, 2),)),
        "out_gain": jnp.clip(1.0 + 0.18 * jax.random.normal(streams_of[7], (D,), jnp.float32), 0.1, 1.9),
    }


ETA_STEP = 0.5
EPSILON = 1e-06

def silu_pair(gate_pre):
    sigmoid_val = jax.nn.sigmoid(gate_pre)
    return (gate_pre * sigmoid_val, sigmoid_val * (1.0 + gate_pre * (1.0 - sigmoid_val)))

def inner_rows(left_op, right_op):
    return lax.dot_general(left_op, right_op, (((0,), (0,)), ((), ())), preferred_element_type=jnp.float32)

def outer_cols(left_op, right_op):
    return lax.dot_general(left_op, right_op, (((1,), (1,)), ((), ())), preferred_element_type=jnp.float32)

def window_attend(query_block, key_window, value_window, query_pos, key_pos):
    count_q = query_block.shape[0]
    count_k = key_window.shape[0]
    heads_here = query_block.shape[1] // ATT_DIM
    query_heads = query_block.astype(jnp.float32).reshape(count_q, heads_here, ATT_DIM)
    key_heads = key_window.astype(jnp.float32).reshape(count_k, heads_here, ATT_DIM)
    value_heads = value_window.astype(jnp.float32).reshape(count_k, heads_here, ATT_DIM)
    scores = jnp.einsum('qhd,khd->hqk', query_heads, key_heads) * ATT_DIM ** (-0.5)
    allowed = (key_pos[None, :] <= query_pos[:, None]) & (query_pos[:, None] - key_pos[None, :] < WINDOW) & (key_pos[None, :] >= 0)
    weights = jnp.where(allowed[None], jnp.square(jnp.maximum(scores, 0.0)), 0.0).astype(jnp.bfloat16)
    mixed_out = jnp.einsum('hqk,khd->qhd', weights.astype(jnp.float32), value_heads)
    counts = jnp.minimum(query_pos + 1, WINDOW).astype(jnp.float32)
    return mixed_out.reshape(count_q, heads_here * ATT_DIM) / counts[:, None]

def local_grads(key_rows, value_rows, rate_col, gate_w, up_w, down_w):
    gate_pre = jnp.dot(key_rows, gate_w, preferred_element_type=jnp.float32)
    up_pre = jnp.dot(key_rows, up_w, preferred_element_type=jnp.float32)
    activated, derivative = silu_pair(gate_pre)
    hidden = (activated * up_pre).astype(jnp.bfloat16)
    target = (rate_col * value_rows.astype(jnp.float32)).astype(jnp.bfloat16)
    grad_down = inner_rows(hidden, target)
    backward = outer_cols(target, down_w)
    grad_gate = inner_rows(key_rows, (backward * up_pre * derivative).astype(jnp.bfloat16))
    grad_up = inner_rows(key_rows, (backward * activated).astype(jnp.bfloat16))
    return (grad_gate, grad_up, grad_down)

def step_weight(weight_part, gradient, square_sum, count_all, weight_full):
    full_float = weight_full.astype(jnp.float32)
    weight_rms = jnp.sqrt(jnp.mean(jnp.square(full_float)))
    grad_rms = jnp.sqrt(square_sum / count_all + EPSILON)
    return (weight_part.astype(jnp.float32) + ETA_STEP * weight_rms * gradient / grad_rms).astype(jnp.bfloat16)

def apply_fast(query_rows, gate_w, up_w, down_w):
    gate_pre = jnp.dot(query_rows, gate_w, preferred_element_type=jnp.float32)
    up_pre = jnp.dot(query_rows, up_w, preferred_element_type=jnp.float32)
    activated, derivative = silu_pair(gate_pre)
    hidden = (activated * up_pre).astype(jnp.bfloat16)
    return jnp.dot(hidden, down_w, preferred_element_type=jnp.float32)

def reference(queries, keys, values, rates, w_gate, w_up, w_down, out_gain):
    reach_count = (WINDOW + TOK_DEV - 1) // TOK_DEV
    lead_rows = reach_count * TOK_DEV
    combined_list = []
    gate_list = []
    up_list = []
    down_list = []
    for group_index in range(N_HEAD):
        col_low = group_index * FW_DIM
        query_g = queries[:, col_low:col_low + FW_DIM]
        key_g = keys[:, col_low:col_low + FW_DIM]
        value_g = values[:, col_low:col_low + FW_DIM]
        key_pad = jnp.concatenate([jnp.zeros((lead_rows, FW_DIM), jnp.bfloat16), key_g], axis=0)
        value_pad = jnp.concatenate([jnp.zeros((lead_rows, FW_DIM), jnp.bfloat16), value_g], axis=0)

        def block_attend(block_index):
            first_row = (block_index * TOK_DEV).astype(jnp.int32)
            query_block = lax.dynamic_slice_in_dim(query_g, first_row, TOK_DEV, 0)
            key_window = lax.dynamic_slice_in_dim(key_pad, first_row, lead_rows + TOK_DEV, 0)
            value_window = lax.dynamic_slice_in_dim(value_pad, first_row, lead_rows + TOK_DEV, 0)
            query_pos = first_row + jnp.arange(TOK_DEV, dtype=jnp.int32)
            key_pos = first_row - lead_rows + jnp.arange(lead_rows + TOK_DEV, dtype=jnp.int32)
            return window_attend(query_block, key_window, value_window, query_pos, key_pos)
        attended = lax.map(block_attend, jnp.arange(N_SEQ, dtype=jnp.int32)).reshape(TOKENS, FW_DIM)
        gate_w = w_gate[col_low:col_low + FW_DIM]
        up_w = w_up[col_low:col_low + FW_DIM]
        down_w = w_down[group_index * HIDDEN_SIZE:(group_index + 1) * HIDDEN_SIZE]
        rate_col = rates[:, group_index:group_index + 1]
        grad_gate, grad_up, grad_down = local_grads(key_g, value_g, rate_col, gate_w, up_w, down_w)
        new_gate = step_weight(gate_w, grad_gate, jnp.sum(jnp.square(grad_gate)), gate_w.size, gate_w)
        new_up = step_weight(up_w, grad_up, jnp.sum(jnp.square(grad_up)), up_w.size, up_w)
        new_down = step_weight(down_w, grad_down, jnp.sum(jnp.square(grad_down)), down_w.size, down_w)
        applied = apply_fast(query_g, new_gate, new_up, new_down)
        combined_list.append(attended + applied)
        gate_list.append(new_gate)
        up_list.append(new_up)
        down_list.append(new_down)
    combined = jnp.concatenate(combined_list, axis=1)
    square_sum = lax.optimization_barrier(jnp.sum(jnp.square(combined), axis=1, keepdims=True))
    output = (combined * lax.rsqrt(square_sum / D + EPSILON) * out_gain[None, :]).astype(jnp.bfloat16)
    return (output, jnp.concatenate(gate_list, axis=0), jnp.concatenate(up_list, axis=0), jnp.concatenate(down_list, axis=0))
```

```python
import functools

import jax
import jax.numpy as jnp
from jax import lax
from jax.experimental import pallas as pl
from jax.experimental.pallas import tpu as pltpu
from jax.sharding import PartitionSpec as P

ATT_DIM = 128
WINDOW = 512
BLOCK = 256
SUBROWS = 16
CHUNKS = 2


ETA_STEP = 0.5
EPSILON = 1e-06

F32 = jnp.float32
BF16 = jnp.bfloat16
VMEM_LIMIT = 50 * 1024 * 1024


def inner_rows(left_op, right_op):
    return lax.dot_general(
        left_op, right_op, (((0,), (0,)), ((), ())), preferred_element_type=F32
    )


def outer_cols(left_op, right_op):
    return lax.dot_general(
        left_op, right_op, (((1,), (1,)), ((), ())), preferred_element_type=F32
    )


def dot(left_op, right_op):
    return jnp.dot(left_op, right_op, preferred_element_type=F32)


def kernel_call(body, name, out_shape, flops, moved):
    return pl.pallas_call(
        body,
        out_shape=out_shape,
        name=name,
        compiler_params=pltpu.CompilerParams(vmem_limit_bytes=VMEM_LIMIT),
        cost_estimate=pl.CostEstimate(flops=flops, bytes_accessed=moved, transcendentals=0),
    )


def halving_masks(peers, rows):
    bits = []
    while peers % (2 << len(bits)) == 0 and peers > 1 << len(bits):
        bits.append(1 << len(bits))
    pairs = [(b, b) for b in bits]
    if len(bits) >= 3:
        pairs = [(bits[0], bits[1]), (bits[2], bits[2]), (bits[1], bits[0])]
        pairs += [(b, b) for b in bits[3:]]
    steps = []
    while pairs and rows % (2 * SUBROWS) == 0:
        steps.append(pairs.pop(0))
        rows //= 2
    return steps


def mask_here(masks):
    return jnp.where(lax.axis_index("head") % 2 == 0, masks[0], masks[1])


def bit_here(masks):
    return ((lax.axis_index("seq") & mask_here(masks)) != 0).astype(jnp.int32)


def swap(x, masks):
    peers, heads = lax.axis_size("seq"), lax.axis_size("head")
    pairs = [
        (s * heads + h, (s ^ masks[h % 2]) * heads + h)
        for s in range(peers)
        for h in range(heads)
    ]
    return lax.ppermute(x, ("seq", "head"), pairs)


def grads_kernel(k_ref, v_ref, rate_ref, gate_ref, up_ref, down_ref, out_ref):
    rows = k_ref.shape[0]
    key_rows = k_ref[...]
    gate_pre = dot(key_rows, gate_ref[...])
    up_pre = dot(key_rows, up_ref[...])
    sigmoid_val = jax.nn.sigmoid(gate_pre)
    activated = gate_pre * sigmoid_val
    hidden = (activated * up_pre).astype(BF16)
    rate_col = jnp.transpose(jnp.broadcast_to(rate_ref[...], (8, rows)))[:, :1]
    target = (rate_col * v_ref[...].astype(F32)).astype(BF16)
    out_ref[2] = inner_rows(hidden, target)
    backward = outer_cols(target, down_ref[...])
    out_ref[1] = inner_rows(key_rows, (backward * activated).astype(BF16))
    derivative = sigmoid_val * (1.0 + gate_pre * (1.0 - sigmoid_val))
    out_ref[0] = inner_rows(key_rows, (backward * up_pre * derivative).astype(BF16))


def attend_kernel(q_ref, k_ref, v_ref, prev_ref, gate_ref, up_ref, down_ref, out_ref, square_ref):
    rows = q_ref.shape[0]
    reach = WINDOW // BLOCK
    row_at = lax.broadcasted_iota(jnp.int32, (BLOCK, BLOCK), 0)
    col_at = lax.broadcasted_iota(jnp.int32, (BLOCK, BLOCK), 1)
    first = lax.axis_index("seq") * rows
    for block in range(rows // BLOCK):
        here = slice(block * BLOCK, (block + 1) * BLOCK)
        position = first + block * BLOCK + lax.broadcasted_iota(jnp.int32, (BLOCK, 1), 0)
        counts = jnp.minimum(position + 1, WINDOW).astype(F32)
        scale = 1.0 / (counts * ATT_DIM)
        for col in range(0, q_ref.shape[1], ATT_DIM):
            cols = slice(col, col + ATT_DIM)
            query = q_ref[here, cols]
            total = None
            for other in range(block - reach, block + 1):
                if other < 0:
                    there = slice((other + reach) * BLOCK, (other + reach + 1) * BLOCK)
                    key, value = prev_ref[0, there, cols], prev_ref[1, there, cols]
                else:
                    there = slice(other * BLOCK, (other + 1) * BLOCK)
                    key, value = k_ref[there, cols], v_ref[there, cols]
                score = jnp.maximum(outer_cols(query, key), 0.0)
                weight = score * score
                if other == block:
                    weight = jnp.where(col_at <= row_at, weight, 0.0)
                if other == block - reach:
                    weight = jnp.where(col_at > row_at, weight, 0.0)
                part = dot(weight.astype(BF16), value)
                total = part if total is None else total + part
            out_ref[here, cols] = total * scale
    for at, ref in enumerate((gate_ref, up_ref, down_ref)):
        whole = jnp.square(ref[...].astype(F32))
        square_ref[at] = jnp.sum(whole.reshape(-1, 8, whole.shape[1]), axis=0)


def apply_kernel(steps, part_rows, *refs):
    count = 2 * CHUNKS if steps else CHUNKS
    pieces, refs = refs[:count], refs[count:]
    q_ref, gate_ref, up_ref, down_ref, square_ref, attended_ref = refs[:6]
    combined_ref, sums_ref, next_gate_ref, next_up_ref, next_down_ref = refs[6:11]
    next_refs = refs[11:]
    bits = [bit_here(m) for m in steps]
    seq_index = lax.axis_index("seq")
    for at, (old_ref, new_ref) in enumerate(zip((gate_ref, up_ref, down_ref), next_refs)):
        size = old_ref.shape[0] * old_ref.shape[1]
        chunk_rows = old_ref.shape[0] // CHUNKS
        total = None
        for piece in pieces:
            part = jnp.square(piece[at].astype(F32))
            part = jnp.sum(part.reshape(-1, 8, part.shape[1]), axis=0)
            total = part if total is None else total + part
        grad_rms = jnp.sqrt(jnp.sum(total, keepdims=True) / size + EPSILON)
        weight_rms = jnp.sqrt(jnp.sum(square_ref[at], keepdims=True) / size)
        factor = ETA_STEP * weight_rms / grad_rms
        if not steps:
            for chunk, piece in enumerate(pieces):
                here = slice(chunk * chunk_rows, (chunk + 1) * chunk_rows)
                new_ref[here] = (old_ref[here].astype(F32) + factor * piece[at].astype(F32)).astype(BF16)
            continue
        unit = chunk_rows >> len(steps)
        for chunk in range(CHUNKS):
            for arrived in range(2):
                piece = pieces[2 * chunk + arrived]
                for block in range(piece.shape[1] // unit):
                    start = chunk * chunk_rows
                    for p, bit in enumerate(bits):
                        came = arrived if p == 0 else (block >> (len(steps) - 1 - p)) & 1
                        start = start + (bit ^ came) * (chunk_rows >> (p + 1))
                    there = pl.ds(pl.multiple_of(start, unit), unit)
                    grad = piece[at, block * unit : (block + 1) * unit].astype(F32)
                    new_ref[there] = (old_ref[there].astype(F32) + factor * grad).astype(BF16)
    for new_ref, part_ref in zip(next_refs, (next_gate_ref, next_up_ref, next_down_ref)):
        kept = part_ref.shape[0]
        start = (seq_index * part_rows) // kept * kept
        part_ref[...] = new_ref[pl.ds(pl.multiple_of(start, kept), kept)]
    ones = jnp.ones((8, attended_ref.shape[1]), BF16)
    for block in range(q_ref.shape[0] // BLOCK):
        here = slice(block * BLOCK, (block + 1) * BLOCK)
        query = q_ref[here]
        gate_pre = dot(query, next_refs[0][...])
        up_pre = dot(query, next_refs[1][...])
        hidden = (gate_pre * jax.nn.sigmoid(gate_pre) * up_pre).astype(BF16)
        combined = attended_ref[here] + dot(hidden, next_refs[2][...])
        combined_ref[here] = combined
        squares = combined * combined
        high = squares.astype(BF16)
        low = (squares - high.astype(F32)).astype(BF16)
        sums_ref[:, here] = outer_cols(ones, high) + outer_cols(ones, low)


def norm_kernel(width, combined_ref, sums_ref, more_ref, gain_ref, out_ref):
    sums = sums_ref[...] if more_ref is None else sums_ref[...] + more_ref[...]
    scale = jnp.transpose(lax.rsqrt(sums / width + EPSILON))[:, :1]
    out_ref[...] = (combined_ref[...] * scale * gain_ref[...]).astype(BF16)


def body(queries, keys, values, rates, w_gate, w_up, w_down, out_gain):
    tok_rows, fw_dim = queries.shape
    seq_count, head_count = lax.axis_size("seq"), lax.axis_size("head")
    w_rows, w_cols = w_gate.shape
    weights = (w_gate, w_up, w_down)

    tail = jnp.stack([keys, values])[:, tok_rows - WINDOW :]
    prev = lax.ppermute(tail, "seq", [(i, i + 1) for i in range(seq_count - 1)])

    grads = kernel_call(
        grads_kernel,
        "gradients",
        jax.ShapeDtypeStruct((3, w_rows, w_cols), F32),
        12 * tok_rows * fw_dim * w_cols,
        8 * tok_rows * fw_dim,
    )(keys, values, rates.reshape(1, tok_rows), *weights)

    chunk_rows = w_rows // CHUNKS
    steps = halving_masks(seq_count, chunk_rows)
    chunks = [grads[:, c * chunk_rows : (c + 1) * chunk_rows] for c in range(CHUNKS)]
    for masks in steps:
        bit = bit_here(masks)
        halves = []
        for g in chunks:
            half = g.shape[1] // 2
            kept = lax.dynamic_slice_in_dim(g, bit * half, half, 1)
            sent = lax.dynamic_slice_in_dim(g, (1 - bit) * half, half, 1).astype(BF16)
            halves.append(kept + swap(sent, masks).astype(F32))
        chunks = halves
    if 1 << len(steps) < seq_count:
        used = 0
        for masks in steps:
            used |= masks[0]
        groups = {}
        for s in range(seq_count):
            groups.setdefault(s & used, []).append(s)
        chunks = [lax.psum(g, "seq", axis_index_groups=list(groups.values())) for g in chunks]
    chunks = [g.astype(BF16) for g in chunks]
    for masks in steps[:0:-1]:
        chunks = [jnp.concatenate([g, swap(g, masks)], axis=1) for g in chunks]
    pieces = []
    for g in chunks:
        pieces.append(g)
        if steps:
            pieces.append(swap(g, steps[0]))

    attended, squares = kernel_call(
        attend_kernel,
        "window_attention",
        (
            jax.ShapeDtypeStruct((tok_rows, fw_dim), F32),
            jax.ShapeDtypeStruct((3, 8, w_cols), F32),
        ),
        4 * tok_rows * (WINDOW + BLOCK) * fw_dim,
        8 * tok_rows * fw_dim,
    )(queries, keys, values, prev, *weights)

    part_rows = w_rows // seq_count
    kept_rows = max(part_rows, SUBROWS)
    part_shape = jax.ShapeDtypeStruct((kept_rows, w_cols), BF16)
    combined, sums, *parts = pl.pallas_call(
        functools.partial(apply_kernel, steps, part_rows),
        out_shape=(
            jax.ShapeDtypeStruct((tok_rows, fw_dim), F32),
            jax.ShapeDtypeStruct((8, tok_rows), F32),
            part_shape,
            part_shape,
            part_shape,
        ),
        name="apply",
        scratch_shapes=[pltpu.VMEM((w_rows, w_cols), BF16)] * 3,
        compiler_params=pltpu.CompilerParams(vmem_limit_bytes=VMEM_LIMIT),
        cost_estimate=pl.CostEstimate(
            flops=6 * tok_rows * fw_dim * w_cols,
            bytes_accessed=12 * tok_rows * fw_dim,
            transcendentals=0,
        ),
    )(*pieces, queries, *weights, squares, attended)
    if part_rows < kept_rows:
        start = (lax.axis_index("seq") * part_rows) % kept_rows
        parts = [lax.dynamic_slice_in_dim(p, start, part_rows, 0) for p in parts]

    width = fw_dim * head_count
    if head_count == 2:
        more = [lax.ppermute(sums, "head", [(0, 1), (1, 0)])]
        norm = functools.partial(norm_kernel, width)
    else:
        sums, more = lax.psum(sums, "head"), []

        def norm(combined_ref, sums_ref, gain_ref, out_ref):
            norm_kernel(width, combined_ref, sums_ref, None, gain_ref, out_ref)

    output = kernel_call(
        norm,
        "norm",
        jax.ShapeDtypeStruct((tok_rows, fw_dim), BF16),
        4 * tok_rows * fw_dim,
        6 * tok_rows * fw_dim,
    )(combined, sums, *more, out_gain.reshape(1, fw_dim))
    return (output, *parts)


def solution(mesh):
    placed = (
        P("seq", "head"),
        P("seq", "head"),
        P("seq", "head"),
        P("seq", "head"),
        P("head", None),
        P("head", None),
        P("head", None),
        P("head"),
    )
    return jax.shard_map(
        body,
        mesh=mesh,
        in_specs=placed,
        out_specs=(
            P("seq", "head"),
            P(("head", "seq"), None),
            P(("head", "seq"), None),
            P(("head", "seq"), None),
        ),
        check_vma=False,
    )
```

```python
import functools

import jax
import jax.numpy as jnp
from jax import lax
from jax.experimental import pallas as pl
from jax.experimental.pallas import tpu as pltpu
from jax.sharding import PartitionSpec as P

ATT_DIM = 128
WINDOW = 512
BLOCK = 256
SUBROWS = 16
CHUNKS = 2


ETA_STEP = 0.5
EPSILON = 1e-06

F32 = jnp.float32
BF16 = jnp.bfloat16
VMEM_LIMIT = 40 * 1024 * 1024
VMEM_WHOLE = 62 * 1024 * 1024


def inner_rows(left_op, right_op):
    return lax.dot_general(
        left_op, right_op, (((0,), (0,)), ((), ())), preferred_element_type=F32
    )


def outer_cols(left_op, right_op):
    return lax.dot_general(
        left_op, right_op, (((1,), (1,)), ((), ())), preferred_element_type=F32
    )


def dot(left_op, right_op):
    return jnp.dot(left_op, right_op, preferred_element_type=F32)


def kernel_call(body, name, out_shape, flops, moved):
    return pl.pallas_call(
        body,
        out_shape=out_shape,
        name=name,
        compiler_params=pltpu.CompilerParams(vmem_limit_bytes=VMEM_LIMIT),
        cost_estimate=pl.CostEstimate(flops=flops, bytes_accessed=moved, transcendentals=0),
    )


def exchange_masks(peers):
    bits = [1 << at for at in range(peers.bit_length() - 1)]
    halving = [(bits[1], bits[2]), (bits[2], bits[1]), (bits[0], bits[0])]
    return halving, [(b, b) for b in bits[3:]]


def mask_here(masks):
    return jnp.where(lax.axis_index("head") % 2 == 0, masks[0], masks[1])


def bit_here(masks):
    return ((lax.axis_index("seq") & mask_here(masks)) != 0).astype(jnp.int32)


def swap(x, masks):
    peers, heads = lax.axis_size("seq"), lax.axis_size("head")
    pairs = [
        (s * heads + h, (s ^ masks[h % 2]) * heads + h)
        for s in range(peers)
        for h in range(heads)
    ]
    return lax.ppermute(x, ("seq", "head"), pairs)


def tails_kernel(v_hbm, k_hbm, v_out, k_out, v_ref, k_ref, sems):
    rows = v_ref.shape[0]
    moves = []
    for source, held, target in ((v_hbm, v_ref, v_out), (k_hbm, k_ref, k_out)):
        for start in range(0, rows, BLOCK // 2):
            here = pl.ds(start, BLOCK // 2)
            there = pl.ds(source.shape[0] - rows + start, BLOCK // 2)
            moves.append((source.at[there], held.at[here], target.at[here]))
    first = [pltpu.make_async_copy(a, b, sems.at[0, i]) for i, (a, b, _) in enumerate(moves)]
    second = [pltpu.make_async_copy(b, c, sems.at[1, i]) for i, (_, b, c) in enumerate(moves)]
    for copy in first:
        copy.start()
    for copy, after in zip(first, second):
        copy.wait()
        after.start()
    for after in second:
        after.wait()


def shift_tail(x):
    return lax.ppermute(x, "seq", [(i, i + 1) for i in range(lax.axis_size("seq") - 1)])


def pass_odd(x):
    return lax.ppermute(x, "seq", [(i, i ^ 2) for i in range(1, lax.axis_size("seq"), 2)])


def shift_passed(x, passed):
    peers = lax.axis_size("seq")
    odd = lax.axis_index("seq") % 2 == 1
    pairs = [(i, i + 1) for i in range(0, peers, 2)]
    pairs += [(i, (i ^ 2) + 1) for i in range(1, peers, 2) if (i ^ 2) + 1 < peers]
    return lax.ppermute(jnp.where(odd, passed, x), "seq", pairs)


def grads_kernel(step, *refs):
    k_hbm, v_hbm, gate_hbm, up_hbm, down_hbm, rate_ref = refs[:6]
    sent_refs, kept_refs = refs[6 : 6 + CHUNKS], refs[6 + CHUNKS : 6 + 2 * CHUNKS]
    k_ref, v_ref, gate_ref, up_ref, down_ref, order_ref, hidden_ref, sems = refs[6 + 2 * CHUNKS :]
    copies = [
        pltpu.make_async_copy(source, target, sems.at[at])
        for at, (source, target) in enumerate(
            (
                (k_hbm, k_ref),
                (gate_hbm, gate_ref),
                (up_hbm, up_ref),
                (v_hbm, v_ref),
                (down_hbm, down_ref),
            )
        )
    ]
    for copy in copies:
        copy.start()
    rows = k_ref.shape[0]
    half = sent_refs[0].shape[1]
    bit = bit_here(step)
    places = []
    for chunk in range(CHUNKS):
        for which in (1 - bit, bit):
            start = pl.multiple_of((2 * chunk + which) * half, half)
            places.append(pl.ds(start, half))
    copies[0].wait()
    key_rows = k_ref[...]
    for at, place in enumerate(places):
        order_ref[:, at * half : (at + 1) * half] = k_ref[:, place]
    copies[1].wait()
    gate_pre = dot(key_rows, gate_ref[...])
    copies[2].wait()
    up_pre = dot(key_rows, up_ref[...])
    sigmoid_val = jax.nn.sigmoid(gate_pre)
    activated = gate_pre * sigmoid_val
    hidden_ref[...] = (activated * up_pre).astype(BF16)
    copies[3].wait()
    rate_col = jnp.transpose(jnp.broadcast_to(rate_ref[...], (8, rows)))[:, :1]
    target = (rate_col * v_ref[...].astype(F32)).astype(BF16)
    copies[4].wait()
    backward = outer_cols(target, down_ref[...])
    derivative = sigmoid_val * (1.0 + gate_pre * (1.0 - sigmoid_val))
    d_gate = (backward * up_pre * derivative).astype(BF16)
    d_up = (backward * activated).astype(BF16)

    def put(matrix, product):
        for chunk in range(CHUNKS):
            start = 2 * chunk * half
            sent_refs[chunk][matrix] = product[start : start + half].astype(BF16)
            kept_refs[chunk][matrix] = product[start + half : start + 2 * half]

    ordered = order_ref[...]
    put(0, inner_rows(ordered, d_gate))
    put(1, inner_rows(ordered, d_up))
    for at, place in enumerate(places):
        order_ref[:, at * half : (at + 1) * half] = hidden_ref[:, place]
    put(2, inner_rows(order_ref[...], target))


def fold_kernel(step, *refs):
    sent_ref, next_ref = refs[-2:]
    kept_refs, came_refs = refs[: len(refs) // 2 - 1], refs[len(refs) // 2 - 1 : -2]
    half = sent_ref.shape[1] // len(kept_refs)
    bit = bit_here(step)
    for at, (kept_ref, came_ref) in enumerate(zip(kept_refs, came_refs)):
        there = slice(at * half, (at + 1) * half)
        for which, ref in ((1 - bit, sent_ref), (bit, next_ref)):
            rows = pl.ds(pl.multiple_of(which * half, half), half)
            ref[:, there] = (kept_ref[:, rows] + came_ref[:, rows].astype(F32)).astype(ref.dtype)


def fold(step, kept, came):
    rows = sum(k.shape[1] // 2 for k in kept)
    shape = (kept[0].shape[0], rows, kept[0].shape[2])
    size = shape[0] * shape[1] * shape[2]
    return kernel_call(
        functools.partial(fold_kernel, step),
        "fold",
        (jax.ShapeDtypeStruct(shape, BF16), jax.ShapeDtypeStruct(shape, F32)),
        2 * size,
        18 * size,
    )(*kept, *came)


def attend_kernel(q_ref, k_ref, v_ref, prev_k_ref, prev_v_ref, gate_ref, up_ref, down_ref, out_ref, square_ref):
    rows = q_ref.shape[0]
    reach = WINDOW // BLOCK
    row_at = lax.broadcasted_iota(jnp.int32, (BLOCK, BLOCK), 0)
    col_at = lax.broadcasted_iota(jnp.int32, (BLOCK, BLOCK), 1)
    first = lax.axis_index("seq") * rows
    for block in range(rows // BLOCK):
        here = slice(block * BLOCK, (block + 1) * BLOCK)
        position = first + block * BLOCK + lax.broadcasted_iota(jnp.int32, (BLOCK, 1), 0)
        counts = jnp.minimum(position + 1, WINDOW).astype(F32)
        scale = 1.0 / (counts * ATT_DIM)
        for col in range(0, q_ref.shape[1], ATT_DIM):
            cols = slice(col, col + ATT_DIM)
            query = q_ref[here, cols]
            total = None
            for other in range(block - reach, block + 1):
                if other < 0:
                    there = slice((other + reach) * BLOCK, (other + reach + 1) * BLOCK)
                    key, value = prev_k_ref[there, cols], prev_v_ref[there, cols]
                else:
                    there = slice(other * BLOCK, (other + 1) * BLOCK)
                    key, value = k_ref[there, cols], v_ref[there, cols]
                score = jnp.maximum(outer_cols(query, key), 0.0)
                weight = score * score
                if other == block:
                    weight = jnp.where(col_at <= row_at, weight, 0.0)
                if other == block - reach:
                    weight = jnp.where(col_at > row_at, weight, 0.0)
                part = dot(weight.astype(BF16), value)
                total = part if total is None else total + part
            out_ref[here, cols] = total * scale
    for at, ref in enumerate((gate_ref, up_ref, down_ref)):
        whole = jnp.square(ref[...].astype(F32))
        square_ref[at] = jnp.sum(whole.reshape(-1, 8, whole.shape[1]), axis=0)


def apply_kernel(steps, part_rows, *refs):
    count = 2 * CHUNKS
    pieces, refs = refs[:count], refs[count:]
    q_ref, gate_ref, up_ref, down_ref, square_ref, attended_ref = refs[:6]
    combined_ref, sums_ref, next_gate_ref, next_up_ref, next_down_ref = refs[6:11]
    next_refs = refs[11:]
    bits = [bit_here(m) for m in steps]
    seq_index = lax.axis_index("seq")
    for at, (old_ref, new_ref) in enumerate(zip((gate_ref, up_ref, down_ref), next_refs)):
        size = old_ref.shape[0] * old_ref.shape[1]
        chunk_rows = old_ref.shape[0] // CHUNKS
        total = None
        for piece in pieces:
            part = jnp.square(piece[at].astype(F32))
            part = jnp.sum(part.reshape(-1, 8, part.shape[1]), axis=0)
            total = part if total is None else total + part
        grad_rms = jnp.sqrt(jnp.sum(total, keepdims=True) / size + EPSILON)
        weight_rms = jnp.sqrt(jnp.sum(square_ref[at], keepdims=True) / size)
        factor = ETA_STEP * weight_rms / grad_rms
        unit = chunk_rows >> len(steps)
        for chunk in range(CHUNKS):
            for arrived in range(2):
                piece = pieces[2 * chunk + arrived]
                for block in range(piece.shape[1] // unit):
                    start = chunk * chunk_rows
                    for p, bit in enumerate(bits):
                        came = arrived if p == 0 else (block >> (len(steps) - 1 - p)) & 1
                        start = start + (bit ^ came) * (chunk_rows >> (p + 1))
                    there = pl.ds(pl.multiple_of(start, unit), unit)
                    grad = piece[at, block * unit : (block + 1) * unit].astype(F32)
                    new_ref[there] = (old_ref[there].astype(F32) + factor * grad).astype(BF16)
    for new_ref, part_ref in zip(next_refs, (next_gate_ref, next_up_ref, next_down_ref)):
        kept = part_ref.shape[0]
        start = (seq_index * part_rows) // kept * kept
        part_ref[...] = new_ref[pl.ds(pl.multiple_of(start, kept), kept)]
    ones = jnp.ones((8, attended_ref.shape[1]), BF16)
    for block in range(q_ref.shape[0] // BLOCK):
        here = slice(block * BLOCK, (block + 1) * BLOCK)
        query = q_ref[here]
        gate_pre = dot(query, next_refs[0][...])
        up_pre = dot(query, next_refs[1][...])
        hidden = (gate_pre * jax.nn.sigmoid(gate_pre) * up_pre).astype(BF16)
        combined = attended_ref[here] + dot(hidden, next_refs[2][...])
        combined_ref[here] = combined
        squares = combined * combined
        high = squares.astype(BF16)
        low = (squares - high.astype(F32)).astype(BF16)
        sums_ref[:, here] = outer_cols(ones, high) + outer_cols(ones, low)


def norm_kernel(width, combined_ref, sums_ref, more_ref, gain_ref, out_ref):
    sums = sums_ref[...] if more_ref is None else sums_ref[...] + more_ref[...]
    scale = jnp.transpose(lax.rsqrt(sums / width + EPSILON))[:, :1]
    out_ref[...] = (combined_ref[...] * scale * gain_ref[...]).astype(BF16)


def body(queries, keys, values, rates, w_gate, w_up, w_down, out_gain):
    tok_rows, fw_dim = queries.shape
    seq_count, head_count = lax.axis_size("seq"), lax.axis_size("head")
    w_rows, w_cols = w_gate.shape
    weights = (w_gate, w_up, w_down)

    hbm = pl.BlockSpec(memory_space=pltpu.HBM)
    tail_shape = jax.ShapeDtypeStruct((WINDOW, fw_dim), BF16)
    value_tail, key_tail = pl.pallas_call(
        tails_kernel,
        out_shape=(tail_shape, tail_shape),
        in_specs=[hbm, hbm],
        out_specs=(hbm, hbm),
        name="tails",
        scratch_shapes=[
            pltpu.VMEM((WINDOW, fw_dim), BF16),
            pltpu.VMEM((WINDOW, fw_dim), BF16),
            pltpu.SemaphoreType.DMA((2, 4 * WINDOW // BLOCK)),
        ],
        compiler_params=pltpu.CompilerParams(vmem_limit_bytes=VMEM_WHOLE),
    )(values, keys)
    prev_keys, passed = shift_tail(key_tail), pass_odd(value_tail)

    chunk_rows = w_rows // CHUNKS
    steps, others = exchange_masks(seq_count)
    half = chunk_rows // 2
    parts = pl.pallas_call(
        functools.partial(grads_kernel, steps[0]),
        out_shape=[jax.ShapeDtypeStruct((3, half, w_cols), BF16)] * CHUNKS
        + [jax.ShapeDtypeStruct((3, half, w_cols), F32)] * CHUNKS,
        in_specs=[hbm] * 5 + [pl.BlockSpec(memory_space=pltpu.VMEM)],
        name="gradients",
        scratch_shapes=[
            pltpu.VMEM(keys.shape, BF16),
            pltpu.VMEM(values.shape, BF16),
            pltpu.VMEM(w_gate.shape, BF16),
            pltpu.VMEM(w_up.shape, BF16),
            pltpu.VMEM(w_down.shape, BF16),
            pltpu.VMEM(keys.shape, BF16),
            pltpu.VMEM((tok_rows, w_cols), BF16),
            pltpu.SemaphoreType.DMA((5,)),
        ],
        compiler_params=pltpu.CompilerParams(vmem_limit_bytes=VMEM_WHOLE),
        cost_estimate=pl.CostEstimate(
            flops=12 * tok_rows * fw_dim * w_cols,
            bytes_accessed=16 * tok_rows * fw_dim,
            transcendentals=0,
        ),
    )(keys, values, *weights, rates.reshape(1, tok_rows))
    sent, kept = parts[:CHUNKS], parts[CHUNKS:]
    came = [swap(x, steps[0]) for x in sent]
    came[0], prev_keys, passed = lax.optimization_barrier((came[0], prev_keys, passed))
    prev_values = shift_passed(value_tail, passed)
    folded = [fold(steps[1], [k], [c]) for k, c in zip(kept, came)]
    came = [swap(x, steps[1]) for x, _ in folded]
    sent, kept = fold(steps[2], [k for _, k in folded], came)
    came, prev_values = lax.optimization_barrier((swap(sent, steps[2]), prev_values))
    total = kept + came.astype(F32)
    for masks in others:
        total = total.astype(BF16)
        total = total.astype(F32) + swap(total, masks).astype(F32)
    total = total.astype(BF16)
    more = swap(total, steps[2])
    rows = total.shape[1] // CHUNKS
    pieces = []
    for c in range(CHUNKS):
        here = slice(c * rows, (c + 1) * rows)
        piece = jnp.concatenate([total[:, here], more[:, here]], axis=1)
        piece = jnp.concatenate([piece, swap(piece, steps[1])], axis=1)
        pieces += [piece, swap(piece, steps[0])]

    attended, squares = kernel_call(
        attend_kernel,
        "window_attention",
        (
            jax.ShapeDtypeStruct((tok_rows, fw_dim), F32),
            jax.ShapeDtypeStruct((3, 8, w_cols), F32),
        ),
        4 * tok_rows * (WINDOW + BLOCK) * fw_dim,
        8 * tok_rows * fw_dim,
    )(queries, keys, values, prev_keys, prev_values, *weights)

    part_rows = w_rows // seq_count
    kept_rows = max(part_rows, SUBROWS)
    part_shape = jax.ShapeDtypeStruct((kept_rows, w_cols), BF16)
    combined, sums, *parts = pl.pallas_call(
        functools.partial(apply_kernel, steps, part_rows),
        out_shape=(
            jax.ShapeDtypeStruct((tok_rows, fw_dim), F32),
            jax.ShapeDtypeStruct((8, tok_rows), F32),
            part_shape,
            part_shape,
            part_shape,
        ),
        name="apply",
        scratch_shapes=[pltpu.VMEM((w_rows, w_cols), BF16)] * 3,
        compiler_params=pltpu.CompilerParams(vmem_limit_bytes=VMEM_LIMIT),
        cost_estimate=pl.CostEstimate(
            flops=6 * tok_rows * fw_dim * w_cols,
            bytes_accessed=12 * tok_rows * fw_dim,
            transcendentals=0,
        ),
    )(*pieces, queries, *weights, squares, attended)
    if part_rows < kept_rows:
        start = (lax.axis_index("seq") * part_rows) % kept_rows
        parts = [lax.dynamic_slice_in_dim(p, start, part_rows, 0) for p in parts]

    width = fw_dim * head_count
    if head_count == 2:
        more = [lax.ppermute(sums, "head", [(0, 1), (1, 0)])]
        norm = functools.partial(norm_kernel, width)
    else:
        sums, more = lax.psum(sums, "head"), []

        def norm(combined_ref, sums_ref, gain_ref, out_ref):
            norm_kernel(width, combined_ref, sums_ref, None, gain_ref, out_ref)

    output = kernel_call(
        norm,
        "norm",
        jax.ShapeDtypeStruct((tok_rows, fw_dim), BF16),
        4 * tok_rows * fw_dim,
        6 * tok_rows * fw_dim,
    )(combined, sums, *more, out_gain.reshape(1, fw_dim))
    return (output, *parts)


def solution(mesh):
    placed = (
        P("seq", "head"),
        P("seq", "head"),
        P("seq", "head"),
        P("seq", "head"),
        P("head", None),
        P("head", None),
        P("head", None),
        P("head"),
    )
    return jax.shard_map(
        body,
        mesh=mesh,
        in_specs=placed,
        out_specs=(
            P("seq", "head"),
            P(("head", "seq"), None),
            P(("head", "seq"), None),
            P(("head", "seq"), None),
        ),
        check_vma=False,
    )
```

```python
import functools

import jax
import jax.numpy as jnp
from jax import lax
from jax.experimental import pallas as pl
from jax.experimental.pallas import tpu as pltpu
from jax.sharding import PartitionSpec as P

ATT_DIM = 128
WINDOW = 512
BLOCK = 256
SUBROWS = 16
CHUNKS = 2


ETA_STEP = 0.5
EPSILON = 1e-06

F32 = jnp.float32
BF16 = jnp.bfloat16
VMEM_LIMIT = 40 * 1024 * 1024
VMEM_WHOLE = 62 * 1024 * 1024


def inner_rows(left_op, right_op):
    return lax.dot_general(
        left_op, right_op, (((0,), (0,)), ((), ())), preferred_element_type=F32
    )


def outer_cols(left_op, right_op):
    return lax.dot_general(
        left_op, right_op, (((1,), (1,)), ((), ())), preferred_element_type=F32
    )


def dot(left_op, right_op):
    return jnp.dot(left_op, right_op, preferred_element_type=F32)


def kernel_call(body, name, out_shape, flops, moved):
    return pl.pallas_call(
        body,
        out_shape=out_shape,
        name=name,
        compiler_params=pltpu.CompilerParams(vmem_limit_bytes=VMEM_LIMIT),
        cost_estimate=pl.CostEstimate(flops=flops, bytes_accessed=moved, transcendentals=0),
    )


def exchange_masks(peers):
    bits = [1 << at for at in range(peers.bit_length() - 1)]
    halving = [(bits[1], bits[2]), (bits[2], bits[1]), (bits[0], bits[0])]
    return halving, [(b, b) for b in bits[3:]]


def mask_here(masks):
    return jnp.where(lax.axis_index("head") % 2 == 0, masks[0], masks[1])


def bit_here(masks):
    return ((lax.axis_index("seq") & mask_here(masks)) != 0).astype(jnp.int32)


def swap(x, masks):
    peers, heads = lax.axis_size("seq"), lax.axis_size("head")
    pairs = [
        (s * heads + h, (s ^ masks[h % 2]) * heads + h)
        for s in range(peers)
        for h in range(heads)
    ]
    return lax.ppermute(x, ("seq", "head"), pairs)


def trade(x):
    peers = lax.axis_size("seq")
    return lax.ppermute(x, "seq", [(i, i ^ 1) for i in range(peers)])


def pass_on(x):
    return lax.ppermute(x, "seq", [(i, i + 2) for i in range(0, lax.axis_size("seq") - 2, 2)])


def grads_kernel(step, *refs):
    k_hbm, v_hbm, gate_hbm, up_hbm, down_hbm, rate_ref, *tail_hbms = refs[:8]
    outs = refs[8 : 8 + 2 * CHUNKS]
    refs = refs[8 + 2 * CHUNKS :]
    held, refs = refs[: 2 * CHUNKS], refs[2 * CHUNKS :]
    k_ref, v_ref, gate_ref, up_ref, down_ref, order_ref, hidden_ref, target_ref, d_gate_ref, d_up_ref = refs[:10]
    in_sems, tail_sems, out_sems = refs[10:]
    moves = ((k_hbm, k_ref), (gate_hbm, gate_ref), (up_hbm, up_ref), (v_hbm, v_ref), (down_hbm, down_ref))
    copies = [pltpu.make_async_copy(a, b, in_sems.at[at]) for at, (a, b) in enumerate(moves)]
    for copy in copies:
        copy.start()
    rows = k_ref.shape[0]
    half = held[0].shape[1]
    bit = bit_here(step)
    places = []
    for chunk in range(CHUNKS):
        for to in (1 - bit, bit):
            places.append(pl.ds(pl.multiple_of((2 * chunk + to) * half, half), half))
    tail = pl.ds(rows - WINDOW, WINDOW)
    tails = [
        pltpu.make_async_copy(ref.at[tail], tail_hbms[at], tail_sems.at[at])
        for at, ref in enumerate((k_ref, v_ref))
    ]
    copies[0].wait()
    tails[0].start()
    for at, place in enumerate(places):
        order_ref[:, place] = k_ref[:, at * half : (at + 1) * half]
    rate_col = jnp.transpose(jnp.broadcast_to(rate_ref[...], (8, rows)))[:, :1]
    for copy in copies[1:]:
        copy.wait()
    tails[1].start()
    for start in range(0, rows, BLOCK):
        here = slice(start, start + BLOCK)
        gate_pre = dot(k_ref[here], gate_ref[...])
        up_pre = dot(k_ref[here], up_ref[...])
        target = (rate_col[here] * v_ref[here].astype(F32)).astype(BF16)
        target_ref[here] = target
        backward = outer_cols(target, down_ref[...])
        sigmoid_val = jax.nn.sigmoid(gate_pre)
        activated = gate_pre * sigmoid_val
        hidden = (activated * up_pre).astype(BF16)
        for at, place in enumerate(places):
            hidden_ref[here, place] = hidden[:, at * half : (at + 1) * half]
        d_up_ref[here] = (backward * activated).astype(BF16)
        derivative = sigmoid_val * (1.0 + gate_pre * (1.0 - sigmoid_val))
        d_gate_ref[here] = (backward * up_pre * derivative).astype(BF16)
    results = []
    for matrix, (left, right) in enumerate(
        ((order_ref, d_gate_ref), (order_ref, d_up_ref), (hidden_ref, target_ref))
    ):
        product = inner_rows(left[...], right[...])
        for chunk in range(CHUNKS):
            start = 2 * chunk * half
            held[chunk][matrix] = product[start : start + half].astype(BF16)
            held[CHUNKS + chunk][matrix] = product[start + half : start + 2 * half]
        for at in range(2 * CHUNKS):
            copy = pltpu.make_async_copy(held[at].at[matrix], outs[at].at[matrix], out_sems.at[matrix, at])
            copy.start()
            results.append(copy)
    for copy in tails + results:
        copy.wait()


def fold_kernel(step, *refs):
    sent_ref, next_ref = refs[-2:]
    kept_refs, came_refs = refs[: len(refs) // 2 - 1], refs[len(refs) // 2 - 1 : -2]
    half = sent_ref.shape[1] // len(kept_refs)
    bit = bit_here(step)
    for at, (kept_ref, came_ref) in enumerate(zip(kept_refs, came_refs)):
        there = slice(at * half, (at + 1) * half)
        for which, ref in ((1 - bit, sent_ref), (bit, next_ref)):
            rows = pl.ds(pl.multiple_of(which * half, half), half)
            ref[:, there] = (kept_ref[:, rows] + came_ref[:, rows].astype(F32)).astype(ref.dtype)


def fold(step, kept, came):
    rows = sum(k.shape[1] // 2 for k in kept)
    shape = (kept[0].shape[0], rows, kept[0].shape[2])
    size = shape[0] * shape[1] * shape[2]
    return kernel_call(
        functools.partial(fold_kernel, step),
        "fold",
        (jax.ShapeDtypeStruct(shape, BF16), jax.ShapeDtypeStruct(shape, F32)),
        2 * size,
        18 * size,
    )(*kept, *came)


def attend_kernel(
    q_ref, k_ref, v_ref, odd_k, odd_v, even_k, even_v, gate_ref, up_ref, down_ref, out_ref, square_ref, prev_ref, sems
):
    rows = q_ref.shape[0]
    odd = lax.axis_index("seq") % 2 == 1

    @pl.when(odd)
    def _():
        pltpu.make_async_copy(odd_k, prev_ref.at[0], sems.at[0]).start()
        pltpu.make_async_copy(odd_v, prev_ref.at[1], sems.at[1]).start()

    @pl.when(jnp.logical_not(odd))
    def _():
        pltpu.make_async_copy(even_k, prev_ref.at[0], sems.at[0]).start()
        pltpu.make_async_copy(even_v, prev_ref.at[1], sems.at[1]).start()

    pltpu.make_async_copy(even_k, prev_ref.at[0], sems.at[0]).wait()
    pltpu.make_async_copy(even_v, prev_ref.at[1], sems.at[1]).wait()
    reach = WINDOW // BLOCK
    row_at = lax.broadcasted_iota(jnp.int32, (BLOCK, BLOCK), 0)
    col_at = lax.broadcasted_iota(jnp.int32, (BLOCK, BLOCK), 1)
    first = lax.axis_index("seq") * rows
    for block in range(rows // BLOCK):
        here = slice(block * BLOCK, (block + 1) * BLOCK)
        position = first + block * BLOCK + lax.broadcasted_iota(jnp.int32, (BLOCK, 1), 0)
        counts = jnp.minimum(position + 1, WINDOW).astype(F32)
        scale = 1.0 / (counts * ATT_DIM)
        for col in range(0, q_ref.shape[1], ATT_DIM):
            cols = slice(col, col + ATT_DIM)
            query = q_ref[here, cols]
            total = None
            for other in range(block - reach, block + 1):
                if other < 0:
                    there = slice((other + reach) * BLOCK, (other + reach + 1) * BLOCK)
                    key, value = prev_ref[0, there, cols], prev_ref[1, there, cols]
                else:
                    there = slice(other * BLOCK, (other + 1) * BLOCK)
                    key, value = k_ref[there, cols], v_ref[there, cols]
                score = jnp.maximum(outer_cols(query, key), 0.0)
                weight = score * score
                if other == block:
                    weight = jnp.where(col_at <= row_at, weight, 0.0)
                if other == block - reach:
                    weight = jnp.where(col_at > row_at, weight, 0.0)
                part = dot(weight.astype(BF16), value)
                total = part if total is None else total + part
            out_ref[here, cols] = total * scale
    for at, ref in enumerate((gate_ref, up_ref, down_ref)):
        whole = jnp.square(ref[...].astype(F32))
        square_ref[at] = jnp.sum(whole.reshape(-1, 8, whole.shape[1]), axis=0)


def apply_kernel(steps, part_rows, *refs):
    count = 2 * CHUNKS
    pieces, refs = refs[:count], refs[count:]
    q_ref, gate_ref, up_ref, down_ref, square_ref, attended_ref = refs[:6]
    combined_ref, sums_ref, next_gate_ref, next_up_ref, next_down_ref = refs[6:11]
    next_refs = refs[11:]
    bits = [bit_here(m) for m in steps]
    seq_index = lax.axis_index("seq")
    for at, (old_ref, new_ref) in enumerate(zip((gate_ref, up_ref, down_ref), next_refs)):
        size = old_ref.shape[0] * old_ref.shape[1]
        chunk_rows = old_ref.shape[0] // CHUNKS
        total = None
        for piece in pieces:
            part = jnp.square(piece[at].astype(F32))
            part = jnp.sum(part.reshape(-1, 8, part.shape[1]), axis=0)
            total = part if total is None else total + part
        grad_rms = jnp.sqrt(jnp.sum(total, keepdims=True) / size + EPSILON)
        weight_rms = jnp.sqrt(jnp.sum(square_ref[at], keepdims=True) / size)
        factor = ETA_STEP * weight_rms / grad_rms
        unit = chunk_rows >> len(steps)
        for chunk in range(CHUNKS):
            for arrived in range(2):
                piece = pieces[2 * chunk + arrived]
                for block in range(piece.shape[1] // unit):
                    start = chunk * chunk_rows
                    for p, bit in enumerate(bits):
                        came = arrived if p == 0 else (block >> (len(steps) - 1 - p)) & 1
                        start = start + (bit ^ came) * (chunk_rows >> (p + 1))
                    there = pl.ds(pl.multiple_of(start, unit), unit)
                    grad = piece[at, block * unit : (block + 1) * unit].astype(F32)
                    new_ref[there] = (old_ref[there].astype(F32) + factor * grad).astype(BF16)
    for new_ref, part_ref in zip(next_refs, (next_gate_ref, next_up_ref, next_down_ref)):
        kept = part_ref.shape[0]
        start = (seq_index * part_rows) // kept * kept
        part_ref[...] = new_ref[pl.ds(pl.multiple_of(start, kept), kept)]
    ones = jnp.ones((8, attended_ref.shape[1]), BF16)
    for block in range(q_ref.shape[0] // BLOCK):
        here = slice(block * BLOCK, (block + 1) * BLOCK)
        query = q_ref[here]
        gate_pre = dot(query, next_refs[0][...])
        up_pre = dot(query, next_refs[1][...])
        hidden = (gate_pre * jax.nn.sigmoid(gate_pre) * up_pre).astype(BF16)
        combined = attended_ref[here] + dot(hidden, next_refs[2][...])
        combined_ref[here] = combined
        squares = combined * combined
        high = squares.astype(BF16)
        low = (squares - high.astype(F32)).astype(BF16)
        sums_ref[:, here] = outer_cols(ones, high) + outer_cols(ones, low)


def norm_kernel(width, combined_ref, sums_ref, more_ref, gain_ref, out_ref):
    sums = sums_ref[...] if more_ref is None else sums_ref[...] + more_ref[...]
    scale = jnp.transpose(lax.rsqrt(sums / width + EPSILON))[:, :1]
    out_ref[...] = (combined_ref[...] * scale * gain_ref[...]).astype(BF16)


def body(queries, keys, values, rates, w_gate, w_up, w_down, out_gain):
    tok_rows, fw_dim = queries.shape
    seq_count, head_count = lax.axis_size("seq"), lax.axis_size("head")
    w_rows, w_cols = w_gate.shape
    weights = (w_gate, w_up, w_down)

    chunk_rows = w_rows // CHUNKS
    steps, others = exchange_masks(seq_count)
    half = chunk_rows // 2
    hbm = pl.BlockSpec(memory_space=pltpu.HBM)
    halves = [((3, half, w_cols), kind) for kind in (BF16, F32) for _ in range(CHUNKS)]
    key_tail, value_tail, *parts = pl.pallas_call(
        functools.partial(grads_kernel, steps[0]),
        out_shape=[jax.ShapeDtypeStruct((WINDOW, fw_dim), BF16)] * 2
        + [jax.ShapeDtypeStruct(*x) for x in halves],
        in_specs=[hbm] * 5 + [pl.BlockSpec(memory_space=pltpu.VMEM)],
        out_specs=[hbm] * (2 + len(halves)),
        name="gradients",
        scratch_shapes=[pltpu.VMEM(*x) for x in halves]
        + [
            pltpu.VMEM(keys.shape, BF16),
            pltpu.VMEM(values.shape, BF16),
            pltpu.VMEM(w_gate.shape, BF16),
            pltpu.VMEM(w_up.shape, BF16),
            pltpu.VMEM(w_down.shape, BF16),
            pltpu.VMEM(keys.shape, BF16),
            pltpu.VMEM((tok_rows, w_cols), BF16),
            pltpu.VMEM(values.shape, BF16),
            pltpu.VMEM((tok_rows, w_cols), BF16),
            pltpu.VMEM((tok_rows, w_cols), BF16),
            pltpu.SemaphoreType.DMA((5,)),
            pltpu.SemaphoreType.DMA((2,)),
            pltpu.SemaphoreType.DMA((3, len(halves))),
        ],
        compiler_params=pltpu.CompilerParams(vmem_limit_bytes=VMEM_WHOLE),
        cost_estimate=pl.CostEstimate(
            flops=12 * tok_rows * fw_dim * w_cols,
            bytes_accessed=16 * tok_rows * fw_dim,
            transcendentals=0,
        ),
    )(keys, values, *weights, rates.reshape(1, tok_rows))
    sent, kept = parts[:CHUNKS], parts[CHUNKS:]
    came = [swap(x, steps[0]) for x in sent]
    beside_k, beside_v = trade(key_tail), trade(value_tail)
    folded = [fold(steps[1], [k], [c]) for k, c in zip(kept, came)]
    came = [swap(x, steps[1]) for x, _ in folded]
    came[0], beside_k = lax.optimization_barrier((came[0], beside_k))
    before_k = pass_on(beside_k)
    sent, kept = fold(steps[2], [k for _, k in folded], came)
    came, beside_v = lax.optimization_barrier((swap(sent, steps[2]), beside_v))
    before_v = pass_on(beside_v)
    total = kept + came.astype(F32)
    for masks in others:
        total = total.astype(BF16)
        came = swap(total, masks)
        if masks == others[-1]:
            came, before_k = lax.optimization_barrier((came, before_k))
        total = total.astype(F32) + came.astype(F32)
    total = total.astype(BF16)
    more, before_v = lax.optimization_barrier((swap(total, steps[2]), before_v))
    rows = total.shape[1] // CHUNKS
    pieces = []
    for c in range(CHUNKS):
        here = slice(c * rows, (c + 1) * rows)
        piece = jnp.concatenate([total[:, here], more[:, here]], axis=1)
        piece = jnp.concatenate([piece, swap(piece, steps[1])], axis=1)
        pieces += [piece, swap(piece, steps[0])]

    attended, squares = pl.pallas_call(
        attend_kernel,
        out_shape=(
            jax.ShapeDtypeStruct((tok_rows, fw_dim), F32),
            jax.ShapeDtypeStruct((3, 8, w_cols), F32),
        ),
        in_specs=[pl.BlockSpec(memory_space=pltpu.VMEM)] * 3
        + [hbm] * 4
        + [pl.BlockSpec(memory_space=pltpu.VMEM)] * 3,
        name="window_attention",
        scratch_shapes=[pltpu.VMEM((2, WINDOW, fw_dim), BF16), pltpu.SemaphoreType.DMA((2,))],
        compiler_params=pltpu.CompilerParams(vmem_limit_bytes=VMEM_LIMIT),
        cost_estimate=pl.CostEstimate(
            flops=4 * tok_rows * (WINDOW + BLOCK) * fw_dim,
            bytes_accessed=8 * tok_rows * fw_dim,
            transcendentals=0,
        ),
    )(queries, keys, values, beside_k, beside_v, before_k, before_v, *weights)

    part_rows = w_rows // seq_count
    kept_rows = max(part_rows, SUBROWS)
    part_shape = jax.ShapeDtypeStruct((kept_rows, w_cols), BF16)
    combined, sums, *parts = pl.pallas_call(
        functools.partial(apply_kernel, steps, part_rows),
        out_shape=(
            jax.ShapeDtypeStruct((tok_rows, fw_dim), F32),
            jax.ShapeDtypeStruct((8, tok_rows), F32),
            part_shape,
            part_shape,
            part_shape,
        ),
        name="apply",
        scratch_shapes=[pltpu.VMEM((w_rows, w_cols), BF16)] * 3,
        compiler_params=pltpu.CompilerParams(vmem_limit_bytes=VMEM_LIMIT),
        cost_estimate=pl.CostEstimate(
            flops=6 * tok_rows * fw_dim * w_cols,
            bytes_accessed=12 * tok_rows * fw_dim,
            transcendentals=0,
        ),
    )(*pieces, queries, *weights, squares, attended)
    if part_rows < kept_rows:
        start = (lax.axis_index("seq") * part_rows) % kept_rows
        parts = [lax.dynamic_slice_in_dim(p, start, part_rows, 0) for p in parts]

    width = fw_dim * head_count
    if head_count == 2:
        more = [lax.ppermute(sums, "head", [(0, 1), (1, 0)])]
        norm = functools.partial(norm_kernel, width)
    else:
        sums, more = lax.psum(sums, "head"), []

        def norm(combined_ref, sums_ref, gain_ref, out_ref):
            norm_kernel(width, combined_ref, sums_ref, None, gain_ref, out_ref)

    output = kernel_call(
        norm,
        "norm",
        jax.ShapeDtypeStruct((tok_rows, fw_dim), BF16),
        4 * tok_rows * fw_dim,
        6 * tok_rows * fw_dim,
    )(combined, sums, *more, out_gain.reshape(1, fw_dim))
    return (output, *parts)


def solution(mesh):
    placed = (
        P("seq", "head"),
        P("seq", "head"),
        P("seq", "head"),
        P("seq", "head"),
        P("head", None),
        P("head", None),
        P("head", None),
        P("head"),
    )
    return jax.shard_map(
        body,
        mesh=mesh,
        in_specs=placed,
        out_specs=(
            P("seq", "head"),
            P(("head", "seq"), None),
            P(("head", "seq"), None),
            P(("head", "seq"), None),
        ),
        check_vma=False,
    )
```

```python
import functools

import jax
import jax.numpy as jnp
from jax import lax
from jax.experimental import pallas as pl
from jax.experimental.pallas import tpu as pltpu
from jax.sharding import PartitionSpec as P

ATT_DIM = 128
WINDOW = 512
BLOCK = 256
SUBROWS = 16
CHUNKS = 2


ETA_STEP = 0.5
EPSILON = 1e-06

F32 = jnp.float32
BF16 = jnp.bfloat16
VMEM_LIMIT = 40 * 1024 * 1024
VMEM_WHOLE = 62 * 1024 * 1024


def inner_rows(left_op, right_op):
    return lax.dot_general(
        left_op, right_op, (((0,), (0,)), ((), ())), preferred_element_type=F32
    )


def outer_cols(left_op, right_op):
    return lax.dot_general(
        left_op, right_op, (((1,), (1,)), ((), ())), preferred_element_type=F32
    )


def dot(left_op, right_op):
    return jnp.dot(left_op, right_op, preferred_element_type=F32)


def kernel_call(body, name, out_shape, flops, moved):
    return pl.pallas_call(
        body,
        out_shape=out_shape,
        name=name,
        compiler_params=pltpu.CompilerParams(vmem_limit_bytes=VMEM_LIMIT),
        cost_estimate=pl.CostEstimate(flops=flops, bytes_accessed=moved, transcendentals=0),
    )


def exchange_masks(peers):
    bits = [1 << at for at in range(peers.bit_length() - 1)]
    halving = [(bits[1], bits[2]), (bits[2], bits[1]), (bits[0], bits[0])]
    return halving, [(b, b) for b in bits[3:]]


def mask_here(masks):
    return jnp.where(lax.axis_index("head") % 2 == 0, masks[0], masks[1])


def bit_here(masks):
    return ((lax.axis_index("seq") & mask_here(masks)) != 0).astype(jnp.int32)


def swap(x, masks):
    peers, heads = lax.axis_size("seq"), lax.axis_size("head")
    pairs = [
        (s * heads + h, (s ^ masks[h % 2]) * heads + h)
        for s in range(peers)
        for h in range(heads)
    ]
    return lax.ppermute(x, ("seq", "head"), pairs)


def trade(x):
    peers = lax.axis_size("seq")
    return lax.ppermute(x, "seq", [(i, i ^ 1) for i in range(peers)])


def pass_on(x):
    return lax.ppermute(x, "seq", [(i, i + 2) for i in range(0, lax.axis_size("seq") - 2, 2)])


def grads_kernel(step, *refs):
    k_hbm, v_hbm, gate_hbm, up_hbm, down_hbm, rate_ref, *tail_hbms = refs[:8]
    outs = refs[8 : 8 + 2 * CHUNKS]
    refs = refs[8 + 2 * CHUNKS :]
    held, refs = refs[: 2 * CHUNKS], refs[2 * CHUNKS :]
    k_ref, v_ref, gate_ref, up_ref, down_ref, order_ref, hidden_ref, target_ref, d_gate_ref, d_up_ref = refs[:10]
    in_sems, tail_sems, out_sems = refs[10:]
    moves = ((k_hbm, k_ref), (gate_hbm, gate_ref), (up_hbm, up_ref), (v_hbm, v_ref), (down_hbm, down_ref))
    copies = [pltpu.make_async_copy(a, b, in_sems.at[at]) for at, (a, b) in enumerate(moves)]
    for copy in copies:
        copy.start()
    rows = k_ref.shape[0]
    half = held[0].shape[1]
    bit = bit_here(step)
    places = []
    for chunk in range(CHUNKS):
        for to in (1 - bit, bit):
            places.append(pl.ds(pl.multiple_of((2 * chunk + to) * half, half), half))
    tail = pl.ds(rows - WINDOW, WINDOW)
    tails = [
        pltpu.make_async_copy(ref.at[tail], tail_hbms[at], tail_sems.at[at])
        for at, ref in enumerate((k_ref, v_ref))
    ]
    copies[0].wait()
    tails[0].start()
    for at, place in enumerate(places):
        order_ref[:, place] = k_ref[:, at * half : (at + 1) * half]
    rate_col = jnp.transpose(jnp.broadcast_to(rate_ref[...], (8, rows)))[:, :1]
    for copy in copies[1:]:
        copy.wait()
    tails[1].start()
    for start in range(0, rows, BLOCK):
        here = slice(start, start + BLOCK)
        gate_pre = dot(k_ref[here], gate_ref[...])
        up_pre = dot(k_ref[here], up_ref[...])
        target = (rate_col[here] * v_ref[here].astype(F32)).astype(BF16)
        target_ref[here] = target
        backward = outer_cols(target, down_ref[...])
        sigmoid_val = jax.nn.sigmoid(gate_pre)
        activated = gate_pre * sigmoid_val
        hidden = (activated * up_pre).astype(BF16)
        for at, place in enumerate(places):
            hidden_ref[here, place] = hidden[:, at * half : (at + 1) * half]
        d_up_ref[here] = (backward * activated).astype(BF16)
        derivative = sigmoid_val * (1.0 + gate_pre * (1.0 - sigmoid_val))
        d_gate_ref[here] = (backward * up_pre * derivative).astype(BF16)
    results = []
    for matrix, (left, right) in enumerate(
        ((order_ref, d_gate_ref), (order_ref, d_up_ref), (hidden_ref, target_ref))
    ):
        product = inner_rows(left[...], right[...])
        for chunk in range(CHUNKS):
            start = 2 * chunk * half
            held[chunk][matrix] = product[start : start + half].astype(BF16)
            held[CHUNKS + chunk][matrix] = product[start + half : start + 2 * half]
        for at in range(2 * CHUNKS):
            copy = pltpu.make_async_copy(held[at].at[matrix], outs[at].at[matrix], out_sems.at[matrix, at])
            copy.start()
            results.append(copy)
    for copy in tails + results:
        copy.wait()


def fold_kernel(step, *refs):
    sent_ref, next_ref = refs[-2:]
    kept_refs, came_refs = refs[: len(refs) // 2 - 1], refs[len(refs) // 2 - 1 : -2]
    half = sent_ref.shape[1] // len(kept_refs)
    bit = bit_here(step)
    for at, (kept_ref, came_ref) in enumerate(zip(kept_refs, came_refs)):
        there = slice(at * half, (at + 1) * half)
        for which, ref in ((1 - bit, sent_ref), (bit, next_ref)):
            rows = pl.ds(pl.multiple_of(which * half, half), half)
            ref[:, there] = (kept_ref[:, rows] + came_ref[:, rows].astype(F32)).astype(ref.dtype)


def fold(step, kept, came):
    rows = sum(k.shape[1] // 2 for k in kept)
    shape = (kept[0].shape[0], rows, kept[0].shape[2])
    size = shape[0] * shape[1] * shape[2]
    return kernel_call(
        functools.partial(fold_kernel, step),
        "fold",
        (jax.ShapeDtypeStruct(shape, BF16), jax.ShapeDtypeStruct(shape, F32)),
        2 * size,
        18 * size,
    )(*kept, *came)


def attend_kernel(
    q_ref, k_ref, v_ref, odd_k, odd_v, even_k, even_v, gate_ref, up_ref, down_ref, out_ref, square_ref, prev_ref, sems
):
    rows = q_ref.shape[0]
    odd = lax.axis_index("seq") % 2 == 1

    @pl.when(odd)
    def _():
        pltpu.make_async_copy(odd_k, prev_ref.at[0], sems.at[0]).start()
        pltpu.make_async_copy(odd_v, prev_ref.at[1], sems.at[1]).start()

    @pl.when(jnp.logical_not(odd))
    def _():
        pltpu.make_async_copy(even_k, prev_ref.at[0], sems.at[0]).start()
        pltpu.make_async_copy(even_v, prev_ref.at[1], sems.at[1]).start()

    pltpu.make_async_copy(even_k, prev_ref.at[0], sems.at[0]).wait()
    pltpu.make_async_copy(even_v, prev_ref.at[1], sems.at[1]).wait()
    reach = WINDOW // BLOCK
    row_at = lax.broadcasted_iota(jnp.int32, (BLOCK, BLOCK), 0)
    col_at = lax.broadcasted_iota(jnp.int32, (BLOCK, BLOCK), 1)
    first = lax.axis_index("seq") * rows
    for block in range(rows // BLOCK):
        here = slice(block * BLOCK, (block + 1) * BLOCK)
        position = first + block * BLOCK + lax.broadcasted_iota(jnp.int32, (BLOCK, 1), 0)
        counts = jnp.minimum(position + 1, WINDOW).astype(F32)
        scale = 1.0 / (counts * ATT_DIM)
        for col in range(0, q_ref.shape[1], ATT_DIM):
            cols = slice(col, col + ATT_DIM)
            query = q_ref[here, cols]
            total = None
            for other in range(block - reach, block + 1):
                if other < 0:
                    there = slice((other + reach) * BLOCK, (other + reach + 1) * BLOCK)
                    key, value = prev_ref[0, there, cols], prev_ref[1, there, cols]
                else:
                    there = slice(other * BLOCK, (other + 1) * BLOCK)
                    key, value = k_ref[there, cols], v_ref[there, cols]
                score = jnp.maximum(outer_cols(query, key), 0.0)
                weight = score * score
                if other == block:
                    weight = jnp.where(col_at <= row_at, weight, 0.0)
                if other == block - reach:
                    weight = jnp.where(col_at > row_at, weight, 0.0)
                part = dot(weight.astype(BF16), value)
                total = part if total is None else total + part
            out_ref[here, cols] = total * scale
    for at, ref in enumerate((gate_ref, up_ref, down_ref)):
        whole = jnp.square(ref[...].astype(F32))
        square_ref[at] = jnp.sum(whole.reshape(-1, 8, whole.shape[1]), axis=0)


def apply_kernel(steps, part_rows, *refs):
    count = 2 * CHUNKS
    pieces, refs = refs[:count], refs[count:]
    q_ref, gate_ref, up_ref, down_ref, square_ref, attended_ref = refs[:6]
    combined_ref, sums_ref, next_gate_ref, next_up_ref, next_down_ref = refs[6:11]
    next_refs = refs[11:]
    bits = [bit_here(m) for m in steps]
    seq_index = lax.axis_index("seq")
    for at, (old_ref, new_ref) in enumerate(zip((gate_ref, up_ref, down_ref), next_refs)):
        size = old_ref.shape[0] * old_ref.shape[1]
        chunk_rows = old_ref.shape[0] // CHUNKS
        total = None
        for piece in pieces:
            part = jnp.square(piece[at].astype(F32))
            part = jnp.sum(part.reshape(-1, 8, part.shape[1]), axis=0)
            total = part if total is None else total + part
        grad_rms = jnp.sqrt(jnp.sum(total, keepdims=True) / size + EPSILON)
        weight_rms = jnp.sqrt(jnp.sum(square_ref[at], keepdims=True) / size)
        factor = ETA_STEP * weight_rms / grad_rms
        unit = chunk_rows >> len(steps)
        for chunk in range(CHUNKS):
            for arrived in range(2):
                piece = pieces[2 * chunk + arrived]
                for block in range(piece.shape[1] // unit):
                    start = chunk * chunk_rows
                    for p, bit in enumerate(bits):
                        came = arrived if p == 0 else (block >> (len(steps) - 1 - p)) & 1
                        start = start + (bit ^ came) * (chunk_rows >> (p + 1))
                    there = pl.ds(pl.multiple_of(start, unit), unit)
                    grad = piece[at, block * unit : (block + 1) * unit].astype(F32)
                    new_ref[there] = (old_ref[there].astype(F32) + factor * grad).astype(BF16)
    for new_ref, part_ref in zip(next_refs, (next_gate_ref, next_up_ref, next_down_ref)):
        kept = part_ref.shape[0]
        start = (seq_index * part_rows) // kept * kept
        part_ref[...] = new_ref[pl.ds(pl.multiple_of(start, kept), kept)]
    ones = jnp.ones((8, attended_ref.shape[1]), BF16)
    for block in range(q_ref.shape[0] // BLOCK):
        here = slice(block * BLOCK, (block + 1) * BLOCK)
        query = q_ref[here]
        gate_pre = dot(query, next_refs[0][...])
        up_pre = dot(query, next_refs[1][...])
        hidden = (gate_pre * jax.nn.sigmoid(gate_pre) * up_pre).astype(BF16)
        combined = attended_ref[here] + dot(hidden, next_refs[2][...])
        combined_ref[here] = combined
        squares = combined * combined
        high = squares.astype(BF16)
        low = (squares - high.astype(F32)).astype(BF16)
        sums_ref[:, here] = outer_cols(ones, high) + outer_cols(ones, low)


def norm_kernel(width, combined_ref, sums_ref, more_ref, gain_ref, out_ref):
    sums = sums_ref[...] if more_ref is None else sums_ref[...] + more_ref[...]
    scale = jnp.transpose(lax.rsqrt(sums / width + EPSILON))[:, :1]
    out_ref[...] = (combined_ref[...] * scale * gain_ref[...]).astype(BF16)


def body(queries, keys, values, rates, w_gate, w_up, w_down, out_gain):
    tok_rows, fw_dim = queries.shape
    seq_count, head_count = lax.axis_size("seq"), lax.axis_size("head")
    w_rows, w_cols = w_gate.shape
    weights = (w_gate, w_up, w_down)

    chunk_rows = w_rows // CHUNKS
    steps, others = exchange_masks(seq_count)
    half = chunk_rows // 2
    hbm = pl.BlockSpec(memory_space=pltpu.HBM)
    halves = [((3, half, w_cols), kind) for kind in (BF16, F32) for _ in range(CHUNKS)]
    key_tail, value_tail, *parts = pl.pallas_call(
        functools.partial(grads_kernel, steps[0]),
        out_shape=[jax.ShapeDtypeStruct((WINDOW, fw_dim), BF16)] * 2
        + [jax.ShapeDtypeStruct(*x) for x in halves],
        in_specs=[hbm] * 5 + [pl.BlockSpec(memory_space=pltpu.VMEM)],
        out_specs=[hbm] * (2 + len(halves)),
        name="gradients",
        scratch_shapes=[pltpu.VMEM(*x) for x in halves]
        + [
            pltpu.VMEM(keys.shape, BF16),
            pltpu.VMEM(values.shape, BF16),
            pltpu.VMEM(w_gate.shape, BF16),
            pltpu.VMEM(w_up.shape, BF16),
            pltpu.VMEM(w_down.shape, BF16),
            pltpu.VMEM(keys.shape, BF16),
            pltpu.VMEM((tok_rows, w_cols), BF16),
            pltpu.VMEM(values.shape, BF16),
            pltpu.VMEM((tok_rows, w_cols), BF16),
            pltpu.VMEM((tok_rows, w_cols), BF16),
            pltpu.SemaphoreType.DMA((5,)),
            pltpu.SemaphoreType.DMA((2,)),
            pltpu.SemaphoreType.DMA((3, len(halves))),
        ],
        compiler_params=pltpu.CompilerParams(vmem_limit_bytes=VMEM_WHOLE),
        cost_estimate=pl.CostEstimate(
            flops=12 * tok_rows * fw_dim * w_cols,
            bytes_accessed=16 * tok_rows * fw_dim,
            transcendentals=0,
        ),
    )(keys, values, *weights, rates.reshape(1, tok_rows))
    sent, kept = parts[:CHUNKS], parts[CHUNKS:]
    came = [swap(x, steps[0]) for x in sent]
    beside_k, beside_v = trade(key_tail), trade(value_tail)
    folded = [fold(steps[1], [k], [c]) for k, c in zip(kept, came)]
    came = [swap(x, steps[1]) for x, _ in folded]
    came[0], beside_k = lax.optimization_barrier((came[0], beside_k))
    before_k = pass_on(beside_k)
    sent, kept = fold(steps[2], [k for _, k in folded], came)
    came, beside_v = lax.optimization_barrier((swap(sent, steps[2]), beside_v))
    before_v = pass_on(beside_v)
    total = kept + came.astype(F32)
    for masks in others:
        total = total.astype(BF16)
        came = swap(total, masks)
        if masks == others[-1]:
            came, before_k = lax.optimization_barrier((came, before_k))
        total = total.astype(F32) + came.astype(F32)
    total = total.astype(BF16)
    more = swap(total, steps[2])
    rows = total.shape[1] // CHUNKS
    pieces = []
    for c in range(CHUNKS):
        here = slice(c * rows, (c + 1) * rows)
        piece = jnp.concatenate([total[:, here], more[:, here]], axis=1)
        came = swap(piece, steps[1])
        if c == 1:
            came, before_v = lax.optimization_barrier((came, before_v))
        piece = jnp.concatenate([piece, came], axis=1)
        pieces += [piece, swap(piece, steps[0])]

    attended, squares = pl.pallas_call(
        attend_kernel,
        out_shape=(
            jax.ShapeDtypeStruct((tok_rows, fw_dim), F32),
            jax.ShapeDtypeStruct((3, 8, w_cols), F32),
        ),
        in_specs=[pl.BlockSpec(memory_space=pltpu.VMEM)] * 3
        + [hbm] * 4
        + [pl.BlockSpec(memory_space=pltpu.VMEM)] * 3,
        name="window_attention",
        scratch_shapes=[pltpu.VMEM((2, WINDOW, fw_dim), BF16), pltpu.SemaphoreType.DMA((2,))],
        compiler_params=pltpu.CompilerParams(vmem_limit_bytes=VMEM_LIMIT),
        cost_estimate=pl.CostEstimate(
            flops=4 * tok_rows * (WINDOW + BLOCK) * fw_dim,
            bytes_accessed=8 * tok_rows * fw_dim,
            transcendentals=0,
        ),
    )(queries, keys, values, beside_k, beside_v, before_k, before_v, *weights)

    part_rows = w_rows // seq_count
    kept_rows = max(part_rows, SUBROWS)
    part_shape = jax.ShapeDtypeStruct((kept_rows, w_cols), BF16)
    combined, sums, *parts = pl.pallas_call(
        functools.partial(apply_kernel, steps, part_rows),
        out_shape=(
            jax.ShapeDtypeStruct((tok_rows, fw_dim), F32),
            jax.ShapeDtypeStruct((8, tok_rows), F32),
            part_shape,
            part_shape,
            part_shape,
        ),
        name="apply",
        scratch_shapes=[pltpu.VMEM((w_rows, w_cols), BF16)] * 3,
        compiler_params=pltpu.CompilerParams(vmem_limit_bytes=VMEM_LIMIT),
        cost_estimate=pl.CostEstimate(
            flops=6 * tok_rows * fw_dim * w_cols,
            bytes_accessed=12 * tok_rows * fw_dim,
            transcendentals=0,
        ),
    )(*pieces, queries, *weights, squares, attended)
    if part_rows < kept_rows:
        start = (lax.axis_index("seq") * part_rows) % kept_rows
        parts = [lax.dynamic_slice_in_dim(p, start, part_rows, 0) for p in parts]

    width = fw_dim * head_count
    if head_count == 2:
        more = [lax.ppermute(sums, "head", [(0, 1), (1, 0)])]
        norm = functools.partial(norm_kernel, width)
    else:
        sums, more = lax.psum(sums, "head"), []

        def norm(combined_ref, sums_ref, gain_ref, out_ref):
            norm_kernel(width, combined_ref, sums_ref, None, gain_ref, out_ref)

    output = kernel_call(
        norm,
        "norm",
        jax.ShapeDtypeStruct((tok_rows, fw_dim), BF16),
        4 * tok_rows * fw_dim,
        6 * tok_rows * fw_dim,
    )(combined, sums, *more, out_gain.reshape(1, fw_dim))
    return (output, *parts)


def solution(mesh):
    placed = (
        P("seq", "head"),
        P("seq", "head"),
        P("seq", "head"),
        P("seq", "head"),
        P("head", None),
        P("head", None),
        P("head", None),
        P("head"),
    )
    return jax.shard_map(
        body,
        mesh=mesh,
        in_specs=placed,
        out_specs=(
            P("seq", "head"),
            P(("head", "seq"), None),
            P(("head", "seq"), None),
            P(("head", "seq"), None),
        ),
        check_vma=False,
    )
```

```python
import functools

import jax
import jax.numpy as jnp
from jax import lax
from jax.experimental import pallas as pl
from jax.experimental.pallas import tpu as pltpu
from jax.sharding import PartitionSpec as P

ATT_DIM = 128
WINDOW = 512
BLOCK = 256
SUBROWS = 16
CHUNKS = 2


ETA_STEP = 0.5
EPSILON = 1e-06

F32 = jnp.float32
BF16 = jnp.bfloat16
VMEM_LIMIT = 40 * 1024 * 1024
VMEM_WHOLE = 62 * 1024 * 1024


def inner_rows(left_op, right_op):
    return lax.dot_general(
        left_op, right_op, (((0,), (0,)), ((), ())), preferred_element_type=F32
    )


def outer_cols(left_op, right_op):
    return lax.dot_general(
        left_op, right_op, (((1,), (1,)), ((), ())), preferred_element_type=F32
    )


def dot(left_op, right_op):
    return jnp.dot(left_op, right_op, preferred_element_type=F32)


def kernel_call(body, name, out_shape, flops, moved):
    return pl.pallas_call(
        body,
        out_shape=out_shape,
        name=name,
        compiler_params=pltpu.CompilerParams(vmem_limit_bytes=VMEM_LIMIT),
        cost_estimate=pl.CostEstimate(flops=flops, bytes_accessed=moved, transcendentals=0),
    )


def exchange_masks(peers):
    bits = [1 << at for at in range(peers.bit_length() - 1)]
    halving = [(bits[1], bits[2]), (bits[2], bits[1]), (bits[0], bits[0])]
    return halving, [(b, b) for b in bits[3:]]


def mask_here(masks):
    return jnp.where(lax.axis_index("head") % 2 == 0, masks[0], masks[1])


def bit_here(masks):
    return ((lax.axis_index("seq") & mask_here(masks)) != 0).astype(jnp.int32)


def swap(x, masks):
    peers, heads = lax.axis_size("seq"), lax.axis_size("head")
    pairs = [
        (s * heads + h, (s ^ masks[h % 2]) * heads + h)
        for s in range(peers)
        for h in range(heads)
    ]
    return lax.ppermute(x, ("seq", "head"), pairs)


def pass_odd(x):
    return lax.ppermute(x, "seq", [(i, i + 2) for i in range(1, lax.axis_size("seq") - 2, 2)])


def shift_passed(x, passed):
    peers = lax.axis_size("seq")
    odd = lax.axis_index("seq") % 2 == 1
    pairs = [(i, i + 1) for i in range(0, peers, 2)] + [(i, i - 1) for i in range(1, peers, 2)]
    return lax.ppermute(jnp.where(odd, passed, x), "seq", pairs)


def trade(x):
    peers = lax.axis_size("seq")
    return lax.ppermute(x, "seq", [(i, i ^ 1) for i in range(peers)])


def pass_on(x):
    return lax.ppermute(x, "seq", [(i, i + 2) for i in range(0, lax.axis_size("seq") - 2, 2)])


def grads_kernel(step, *refs):
    k_hbm, v_hbm, gate_hbm, up_hbm, down_hbm, rate_ref, *tail_hbms = refs[:8]
    outs = refs[8 : 8 + 2 * CHUNKS]
    refs = refs[8 + 2 * CHUNKS :]
    held, refs = refs[: 2 * CHUNKS], refs[2 * CHUNKS :]
    k_ref, v_ref, gate_ref, up_ref, down_ref, order_ref, hidden_ref, target_ref, d_gate_ref, d_up_ref = refs[:10]
    in_sems, tail_sems, out_sems = refs[10:]
    moves = ((k_hbm, k_ref), (gate_hbm, gate_ref), (up_hbm, up_ref), (v_hbm, v_ref), (down_hbm, down_ref))
    copies = [pltpu.make_async_copy(a, b, in_sems.at[at]) for at, (a, b) in enumerate(moves)]
    for copy in copies:
        copy.start()
    rows = k_ref.shape[0]
    half = held[0].shape[1]
    bit = bit_here(step)
    places = []
    for chunk in range(CHUNKS):
        for to in (1 - bit, bit):
            places.append(pl.ds(pl.multiple_of((2 * chunk + to) * half, half), half))
    tail = pl.ds(rows - WINDOW, WINDOW)
    tails = [
        pltpu.make_async_copy(ref.at[tail], tail_hbms[at], tail_sems.at[at])
        for at, ref in enumerate((k_ref, v_ref))
    ]
    copies[0].wait()
    tails[0].start()
    for at, place in enumerate(places):
        order_ref[:, place] = k_ref[:, at * half : (at + 1) * half]
    rate_col = jnp.transpose(jnp.broadcast_to(rate_ref[...], (8, rows)))[:, :1]
    for copy in copies[1:]:
        copy.wait()
    tails[1].start()
    for start in range(0, rows, BLOCK):
        here = slice(start, start + BLOCK)
        gate_pre = dot(k_ref[here], gate_ref[...])
        up_pre = dot(k_ref[here], up_ref[...])
        target = (rate_col[here] * v_ref[here].astype(F32)).astype(BF16)
        target_ref[here] = target
        backward = outer_cols(target, down_ref[...])
        sigmoid_val = jax.nn.sigmoid(gate_pre)
        activated = gate_pre * sigmoid_val
        hidden = (activated * up_pre).astype(BF16)
        for at, place in enumerate(places):
            hidden_ref[here, place] = hidden[:, at * half : (at + 1) * half]
        d_up_ref[here] = (backward * activated).astype(BF16)
        derivative = sigmoid_val * (1.0 + gate_pre * (1.0 - sigmoid_val))
        d_gate_ref[here] = (backward * up_pre * derivative).astype(BF16)
    results = []
    for matrix, (left, right) in enumerate(
        ((order_ref, d_gate_ref), (order_ref, d_up_ref), (hidden_ref, target_ref))
    ):
        product = inner_rows(left[...], right[...])
        for chunk in range(CHUNKS):
            start = 2 * chunk * half
            held[chunk][matrix] = product[start : start + half].astype(BF16)
            held[CHUNKS + chunk][matrix] = product[start + half : start + 2 * half]
        for at in range(2 * CHUNKS):
            copy = pltpu.make_async_copy(held[at].at[matrix], outs[at].at[matrix], out_sems.at[matrix, at])
            copy.start()
            results.append(copy)
    for copy in tails + results:
        copy.wait()


def fold_kernel(step, *refs):
    sent_ref, next_ref = refs[-2:]
    kept_refs, came_refs = refs[: len(refs) // 2 - 1], refs[len(refs) // 2 - 1 : -2]
    half = sent_ref.shape[1] // len(kept_refs)
    bit = bit_here(step)
    for at, (kept_ref, came_ref) in enumerate(zip(kept_refs, came_refs)):
        there = slice(at * half, (at + 1) * half)
        for which, ref in ((1 - bit, sent_ref), (bit, next_ref)):
            rows = pl.ds(pl.multiple_of(which * half, half), half)
            ref[:, there] = (kept_ref[:, rows] + came_ref[:, rows].astype(F32)).astype(ref.dtype)


def fold(step, kept, came):
    rows = sum(k.shape[1] // 2 for k in kept)
    shape = (kept[0].shape[0], rows, kept[0].shape[2])
    size = shape[0] * shape[1] * shape[2]
    return kernel_call(
        functools.partial(fold_kernel, step),
        "fold",
        (jax.ShapeDtypeStruct(shape, BF16), jax.ShapeDtypeStruct(shape, F32)),
        2 * size,
        18 * size,
    )(*kept, *came)


def attend_kernel(
    q_ref, k_ref, v_ref, odd_k, even_k, prev_v, gate_ref, up_ref, down_ref, out_ref, square_ref, prev_ref, sems
):
    rows = q_ref.shape[0]
    odd = lax.axis_index("seq") % 2 == 1
    value_copy = pltpu.make_async_copy(prev_v, prev_ref.at[1], sems.at[1])
    value_copy.start()

    @pl.when(odd)
    def _():
        pltpu.make_async_copy(odd_k, prev_ref.at[0], sems.at[0]).start()

    @pl.when(jnp.logical_not(odd))
    def _():
        pltpu.make_async_copy(even_k, prev_ref.at[0], sems.at[0]).start()

    pltpu.make_async_copy(even_k, prev_ref.at[0], sems.at[0]).wait()
    value_copy.wait()
    reach = WINDOW // BLOCK
    row_at = lax.broadcasted_iota(jnp.int32, (BLOCK, BLOCK), 0)
    col_at = lax.broadcasted_iota(jnp.int32, (BLOCK, BLOCK), 1)
    first = lax.axis_index("seq") * rows
    for block in range(rows // BLOCK):
        here = slice(block * BLOCK, (block + 1) * BLOCK)
        position = first + block * BLOCK + lax.broadcasted_iota(jnp.int32, (BLOCK, 1), 0)
        counts = jnp.minimum(position + 1, WINDOW).astype(F32)
        scale = 1.0 / (counts * ATT_DIM)
        for col in range(0, q_ref.shape[1], ATT_DIM):
            cols = slice(col, col + ATT_DIM)
            query = q_ref[here, cols]
            total = None
            for other in range(block - reach, block + 1):
                if other < 0:
                    there = slice((other + reach) * BLOCK, (other + reach + 1) * BLOCK)
                    key, value = prev_ref[0, there, cols], prev_ref[1, there, cols]
                else:
                    there = slice(other * BLOCK, (other + 1) * BLOCK)
                    key, value = k_ref[there, cols], v_ref[there, cols]
                score = jnp.maximum(outer_cols(query, key), 0.0)
                weight = score * score
                if other == block:
                    weight = jnp.where(col_at <= row_at, weight, 0.0)
                if other == block - reach:
                    weight = jnp.where(col_at > row_at, weight, 0.0)
                part = dot(weight.astype(BF16), value)
                total = part if total is None else total + part
            out_ref[here, cols] = total * scale
    for at, ref in enumerate((gate_ref, up_ref, down_ref)):
        whole = jnp.square(ref[...].astype(F32))
        square_ref[at] = jnp.sum(whole.reshape(-1, 8, whole.shape[1]), axis=0)


def apply_kernel(steps, part_rows, *refs):
    count = 2 * CHUNKS
    pieces, refs = refs[:count], refs[count:]
    q_ref, gate_ref, up_ref, down_ref, square_ref, attended_ref = refs[:6]
    combined_ref, sums_ref, next_gate_ref, next_up_ref, next_down_ref = refs[6:11]
    next_refs = refs[11:]
    bits = [bit_here(m) for m in steps]
    seq_index = lax.axis_index("seq")
    for at, (old_ref, new_ref) in enumerate(zip((gate_ref, up_ref, down_ref), next_refs)):
        size = old_ref.shape[0] * old_ref.shape[1]
        chunk_rows = old_ref.shape[0] // CHUNKS
        total = None
        for piece in pieces:
            part = jnp.square(piece[at].astype(F32))
            part = jnp.sum(part.reshape(-1, 8, part.shape[1]), axis=0)
            total = part if total is None else total + part
        grad_rms = jnp.sqrt(jnp.sum(total, keepdims=True) / size + EPSILON)
        weight_rms = jnp.sqrt(jnp.sum(square_ref[at], keepdims=True) / size)
        factor = ETA_STEP * weight_rms / grad_rms
        unit = chunk_rows >> len(steps)
        for chunk in range(CHUNKS):
            for arrived in range(2):
                piece = pieces[2 * chunk + arrived]
                for block in range(piece.shape[1] // unit):
                    start = chunk * chunk_rows
                    for p, bit in enumerate(bits):
                        came = arrived if p == 0 else (block >> (len(steps) - 1 - p)) & 1
                        start = start + (bit ^ came) * (chunk_rows >> (p + 1))
                    there = pl.ds(pl.multiple_of(start, unit), unit)
                    grad = piece[at, block * unit : (block + 1) * unit].astype(F32)
                    new_ref[there] = (old_ref[there].astype(F32) + factor * grad).astype(BF16)
    for new_ref, part_ref in zip(next_refs, (next_gate_ref, next_up_ref, next_down_ref)):
        kept = part_ref.shape[0]
        start = (seq_index * part_rows) // kept * kept
        part_ref[...] = new_ref[pl.ds(pl.multiple_of(start, kept), kept)]
    ones = jnp.ones((8, attended_ref.shape[1]), BF16)
    for block in range(q_ref.shape[0] // BLOCK):
        here = slice(block * BLOCK, (block + 1) * BLOCK)
        query = q_ref[here]
        gate_pre = dot(query, next_refs[0][...])
        up_pre = dot(query, next_refs[1][...])
        hidden = (gate_pre * jax.nn.sigmoid(gate_pre) * up_pre).astype(BF16)
        combined = attended_ref[here] + dot(hidden, next_refs[2][...])
        combined_ref[here] = combined
        squares = combined * combined
        high = squares.astype(BF16)
        low = (squares - high.astype(F32)).astype(BF16)
        sums_ref[:, here] = outer_cols(ones, high) + outer_cols(ones, low)


def norm_kernel(width, combined_ref, sums_ref, more_ref, gain_ref, out_ref):
    sums = sums_ref[...] if more_ref is None else sums_ref[...] + more_ref[...]
    scale = jnp.transpose(lax.rsqrt(sums / width + EPSILON))[:, :1]
    out_ref[...] = (combined_ref[...] * scale * gain_ref[...]).astype(BF16)


def body(queries, keys, values, rates, w_gate, w_up, w_down, out_gain):
    tok_rows, fw_dim = queries.shape
    seq_count, head_count = lax.axis_size("seq"), lax.axis_size("head")
    w_rows, w_cols = w_gate.shape
    weights = (w_gate, w_up, w_down)

    chunk_rows = w_rows // CHUNKS
    steps, others = exchange_masks(seq_count)
    half = chunk_rows // 2
    hbm = pl.BlockSpec(memory_space=pltpu.HBM)
    halves = [((3, half, w_cols), kind) for kind in (BF16, F32) for _ in range(CHUNKS)]
    key_tail, value_tail, *parts = pl.pallas_call(
        functools.partial(grads_kernel, steps[0]),
        out_shape=[jax.ShapeDtypeStruct((WINDOW, fw_dim), BF16)] * 2
        + [jax.ShapeDtypeStruct(*x) for x in halves],
        in_specs=[hbm] * 5 + [pl.BlockSpec(memory_space=pltpu.VMEM)],
        out_specs=[hbm] * (2 + len(halves)),
        name="gradients",
        scratch_shapes=[pltpu.VMEM(*x) for x in halves]
        + [
            pltpu.VMEM(keys.shape, BF16),
            pltpu.VMEM(values.shape, BF16),
            pltpu.VMEM(w_gate.shape, BF16),
            pltpu.VMEM(w_up.shape, BF16),
            pltpu.VMEM(w_down.shape, BF16),
            pltpu.VMEM(keys.shape, BF16),
            pltpu.VMEM((tok_rows, w_cols), BF16),
            pltpu.VMEM(values.shape, BF16),
            pltpu.VMEM((tok_rows, w_cols), BF16),
            pltpu.VMEM((tok_rows, w_cols), BF16),
            pltpu.SemaphoreType.DMA((5,)),
            pltpu.SemaphoreType.DMA((2,)),
            pltpu.SemaphoreType.DMA((3, len(halves))),
        ],
        compiler_params=pltpu.CompilerParams(vmem_limit_bytes=VMEM_WHOLE),
        cost_estimate=pl.CostEstimate(
            flops=12 * tok_rows * fw_dim * w_cols,
            bytes_accessed=16 * tok_rows * fw_dim,
            transcendentals=0,
        ),
    )(keys, values, *weights, rates.reshape(1, tok_rows))
    sent, kept = parts[:CHUNKS], parts[CHUNKS:]
    came = [swap(x, steps[0]) for x in sent]
    beside_k = trade(key_tail)
    folded = [fold(steps[1], [k], [c]) for k, c in zip(kept, came)]
    came = [swap(x, steps[1]) for x, _ in folded]
    came[0], beside_k = lax.optimization_barrier((came[0], beside_k))
    before_k = pass_on(beside_k)
    passed = pass_odd(value_tail)
    sent, kept = fold(steps[2], [k for _, k in folded], came)
    came = swap(sent, steps[2])
    total = kept + came.astype(F32)
    for masks in others:
        total = total.astype(BF16)
        came = swap(total, masks)
        total = total.astype(F32) + came.astype(F32)
    total = total.astype(BF16)
    more = swap(total, steps[2])
    rows = total.shape[1] // CHUNKS
    pieces = []
    for c in range(CHUNKS):
        here = slice(c * rows, (c + 1) * rows)
        piece = jnp.concatenate([total[:, here], more[:, here]], axis=1)
        came = swap(piece, steps[1])
        if c == 0:
            came, passed = lax.optimization_barrier((came, passed))
            prev_v = shift_passed(value_tail, passed)
        if c == 1:
            came, before_k = lax.optimization_barrier((came, before_k))
        piece = jnp.concatenate([piece, came], axis=1)
        pieces += [piece, swap(piece, steps[0])]

    attended, squares = pl.pallas_call(
        attend_kernel,
        out_shape=(
            jax.ShapeDtypeStruct((tok_rows, fw_dim), F32),
            jax.ShapeDtypeStruct((3, 8, w_cols), F32),
        ),
        in_specs=[pl.BlockSpec(memory_space=pltpu.VMEM)] * 3
        + [hbm] * 3
        + [pl.BlockSpec(memory_space=pltpu.VMEM)] * 3,
        name="window_attention",
        scratch_shapes=[pltpu.VMEM((2, WINDOW, fw_dim), BF16), pltpu.SemaphoreType.DMA((2,))],
        compiler_params=pltpu.CompilerParams(vmem_limit_bytes=VMEM_LIMIT),
        cost_estimate=pl.CostEstimate(
            flops=4 * tok_rows * (WINDOW + BLOCK) * fw_dim,
            bytes_accessed=8 * tok_rows * fw_dim,
            transcendentals=0,
        ),
    )(queries, keys, values, beside_k, before_k, prev_v, *weights)

    part_rows = w_rows // seq_count
    kept_rows = max(part_rows, SUBROWS)
    part_shape = jax.ShapeDtypeStruct((kept_rows, w_cols), BF16)
    combined, sums, *parts = pl.pallas_call(
        functools.partial(apply_kernel, steps, part_rows),
        out_shape=(
            jax.ShapeDtypeStruct((tok_rows, fw_dim), F32),
            jax.ShapeDtypeStruct((8, tok_rows), F32),
            part_shape,
            part_shape,
            part_shape,
        ),
        name="apply",
        scratch_shapes=[pltpu.VMEM((w_rows, w_cols), BF16)] * 3,
        compiler_params=pltpu.CompilerParams(vmem_limit_bytes=VMEM_LIMIT),
        cost_estimate=pl.CostEstimate(
            flops=6 * tok_rows * fw_dim * w_cols,
            bytes_accessed=12 * tok_rows * fw_dim,
            transcendentals=0,
        ),
    )(*pieces, queries, *weights, squares, attended)
    if part_rows < kept_rows:
        start = (lax.axis_index("seq") * part_rows) % kept_rows
        parts = [lax.dynamic_slice_in_dim(p, start, part_rows, 0) for p in parts]

    width = fw_dim * head_count
    if head_count == 2:
        more = [lax.ppermute(sums, "head", [(0, 1), (1, 0)])]
        norm = functools.partial(norm_kernel, width)
    else:
        sums, more = lax.psum(sums, "head"), []

        def norm(combined_ref, sums_ref, gain_ref, out_ref):
            norm_kernel(width, combined_ref, sums_ref, None, gain_ref, out_ref)

    output = kernel_call(
        norm,
        "norm",
        jax.ShapeDtypeStruct((tok_rows, fw_dim), BF16),
        4 * tok_rows * fw_dim,
        6 * tok_rows * fw_dim,
    )(combined, sums, *more, out_gain.reshape(1, fw_dim))
    return (output, *parts)


def solution(mesh):
    placed = (
        P("seq", "head"),
        P("seq", "head"),
        P("seq", "head"),
        P("seq", "head"),
        P("head", None),
        P("head", None),
        P("head", None),
        P("head"),
    )
    return jax.shard_map(
        body,
        mesh=mesh,
        in_specs=placed,
        out_specs=(
            P("seq", "head"),
            P(("head", "seq"), None),
            P(("head", "seq"), None),
            P(("head", "seq"), None),
        ),
        check_vma=False,
    )
```

```python
import functools

import jax
import jax.numpy as jnp
from jax import lax
from jax.experimental import pallas as pl
from jax.experimental.pallas import tpu as pltpu
from jax.sharding import PartitionSpec as P

ATT_DIM = 128
WINDOW = 512
BLOCK = 256
SUBROWS = 16
CHUNKS = 2


ETA_STEP = 0.5
EPSILON = 1e-06

F32 = jnp.float32
BF16 = jnp.bfloat16
VMEM_LIMIT = 40 * 1024 * 1024
VMEM_WHOLE = 62 * 1024 * 1024


def inner_rows(left_op, right_op):
    return lax.dot_general(
        left_op, right_op, (((0,), (0,)), ((), ())), preferred_element_type=F32
    )


def outer_cols(left_op, right_op):
    return lax.dot_general(
        left_op, right_op, (((1,), (1,)), ((), ())), preferred_element_type=F32
    )


def dot(left_op, right_op):
    return jnp.dot(left_op, right_op, preferred_element_type=F32)


def kernel_call(body, name, out_shape, flops, moved):
    return pl.pallas_call(
        body,
        out_shape=out_shape,
        name=name,
        compiler_params=pltpu.CompilerParams(vmem_limit_bytes=VMEM_LIMIT),
        cost_estimate=pl.CostEstimate(flops=flops, bytes_accessed=moved, transcendentals=0),
    )


def exchange_masks(peers):
    bits = [1 << at for at in range(peers.bit_length() - 1)]
    halving = [(bits[2], bits[1]), (bits[1], bits[2]), (bits[0], bits[0])]
    return halving, [(b, b) for b in bits[3:]]


def mask_here(masks):
    return jnp.where(lax.axis_index("head") % 2 == 0, masks[0], masks[1])


def bit_here(masks):
    return ((lax.axis_index("seq") & mask_here(masks)) != 0).astype(jnp.int32)


def swap(x, masks):
    peers, heads = lax.axis_size("seq"), lax.axis_size("head")
    pairs = [
        (s * heads + h, (s ^ masks[h % 2]) * heads + h)
        for s in range(peers)
        for h in range(heads)
    ]
    return lax.ppermute(x, ("seq", "head"), pairs)


def pass_odd(x):
    return lax.ppermute(x, "seq", [(i, i + 2) for i in range(1, lax.axis_size("seq") - 2, 2)])


def shift_passed(x, passed):
    peers = lax.axis_size("seq")
    odd = lax.axis_index("seq") % 2 == 1
    pairs = [(i, i + 1) for i in range(0, peers, 2)] + [(i, i - 1) for i in range(1, peers, 2)]
    return lax.ppermute(jnp.where(odd, passed, x), "seq", pairs)


def trade(x):
    peers = lax.axis_size("seq")
    return lax.ppermute(x, "seq", [(i, i ^ 1) for i in range(peers)])


def pass_on(x):
    return lax.ppermute(x, "seq", [(i, i + 2) for i in range(0, lax.axis_size("seq") - 2, 2)])


def grads_kernel(step, *refs):
    k_hbm, v_hbm, gate_hbm, up_hbm, down_hbm, rate_ref, *tail_hbms = refs[:8]
    outs = refs[8 : 8 + 2 * CHUNKS]
    refs = refs[8 + 2 * CHUNKS :]
    held, refs = refs[: 2 * CHUNKS], refs[2 * CHUNKS :]
    k_ref, v_ref, gate_ref, up_ref, down_ref, order_ref, hidden_ref, target_ref, d_gate_ref, d_up_ref = refs[:10]
    in_sems, tail_sems, out_sems = refs[10:]
    moves = ((k_hbm, k_ref), (gate_hbm, gate_ref), (up_hbm, up_ref), (v_hbm, v_ref), (down_hbm, down_ref))
    copies = [pltpu.make_async_copy(a, b, in_sems.at[at]) for at, (a, b) in enumerate(moves)]
    for copy in copies:
        copy.start()
    rows = k_ref.shape[0]
    half = held[0].shape[1]
    bit = bit_here(step)
    places = []
    for chunk in range(CHUNKS):
        for to in (1 - bit, bit):
            places.append(pl.ds(pl.multiple_of((2 * chunk + to) * half, half), half))
    tail = pl.ds(rows - WINDOW, WINDOW)
    tails = [
        pltpu.make_async_copy(ref.at[tail], tail_hbms[at], tail_sems.at[at])
        for at, ref in enumerate((k_ref, v_ref))
    ]
    copies[0].wait()
    tails[0].start()
    for at, place in enumerate(places):
        order_ref[:, place] = k_ref[:, at * half : (at + 1) * half]
    rate_col = jnp.transpose(jnp.broadcast_to(rate_ref[...], (8, rows)))[:, :1]
    for copy in copies[1:]:
        copy.wait()
    tails[1].start()
    for start in range(0, rows, BLOCK):
        here = slice(start, start + BLOCK)
        gate_pre = dot(k_ref[here], gate_ref[...])
        up_pre = dot(k_ref[here], up_ref[...])
        target = (rate_col[here] * v_ref[here].astype(F32)).astype(BF16)
        target_ref[here] = target
        backward = outer_cols(target, down_ref[...])
        sigmoid_val = jax.nn.sigmoid(gate_pre)
        activated = gate_pre * sigmoid_val
        hidden = (activated * up_pre).astype(BF16)
        for at, place in enumerate(places):
            hidden_ref[here, place] = hidden[:, at * half : (at + 1) * half]
        d_up_ref[here] = (backward * activated).astype(BF16)
        derivative = sigmoid_val * (1.0 + gate_pre * (1.0 - sigmoid_val))
        d_gate_ref[here] = (backward * up_pre * derivative).astype(BF16)
    results = []
    for matrix, (left, right) in enumerate(
        ((order_ref, d_gate_ref), (order_ref, d_up_ref), (hidden_ref, target_ref))
    ):
        product = inner_rows(left[...], right[...])
        for chunk in range(CHUNKS):
            start = 2 * chunk * half
            held[chunk][matrix] = product[start : start + half].astype(BF16)
            held[CHUNKS + chunk][matrix] = product[start + half : start + 2 * half]
        for at in range(2 * CHUNKS):
            copy = pltpu.make_async_copy(held[at].at[matrix], outs[at].at[matrix], out_sems.at[matrix, at])
            copy.start()
            results.append(copy)
    for copy in tails + results:
        copy.wait()


def fold_kernel(step, *refs):
    sent_ref, next_ref = refs[-2:]
    kept_refs, came_refs = refs[: len(refs) // 2 - 1], refs[len(refs) // 2 - 1 : -2]
    half = sent_ref.shape[1] // len(kept_refs)
    bit = bit_here(step)
    for at, (kept_ref, came_ref) in enumerate(zip(kept_refs, came_refs)):
        there = slice(at * half, (at + 1) * half)
        for which, ref in ((1 - bit, sent_ref), (bit, next_ref)):
            rows = pl.ds(pl.multiple_of(which * half, half), half)
            ref[:, there] = (kept_ref[:, rows] + came_ref[:, rows].astype(F32)).astype(ref.dtype)


def fold(step, kept, came):
    rows = sum(k.shape[1] // 2 for k in kept)
    shape = (kept[0].shape[0], rows, kept[0].shape[2])
    size = shape[0] * shape[1] * shape[2]
    return kernel_call(
        functools.partial(fold_kernel, step),
        "fold",
        (jax.ShapeDtypeStruct(shape, BF16), jax.ShapeDtypeStruct(shape, F32)),
        2 * size,
        18 * size,
    )(*kept, *came)


def attend_kernel(
    q_ref, k_ref, v_ref, odd_k, even_k, prev_v, gate_ref, up_ref, down_ref, out_ref, square_ref, prev_ref, sems
):
    rows = q_ref.shape[0]
    odd = lax.axis_index("seq") % 2 == 1
    value_copy = pltpu.make_async_copy(prev_v, prev_ref.at[1], sems.at[1])
    value_copy.start()

    @pl.when(odd)
    def _():
        pltpu.make_async_copy(odd_k, prev_ref.at[0], sems.at[0]).start()

    @pl.when(jnp.logical_not(odd))
    def _():
        pltpu.make_async_copy(even_k, prev_ref.at[0], sems.at[0]).start()

    pltpu.make_async_copy(even_k, prev_ref.at[0], sems.at[0]).wait()
    value_copy.wait()
    reach = WINDOW // BLOCK
    row_at = lax.broadcasted_iota(jnp.int32, (BLOCK, BLOCK), 0)
    col_at = lax.broadcasted_iota(jnp.int32, (BLOCK, BLOCK), 1)
    first = lax.axis_index("seq") * rows
    for block in range(rows // BLOCK):
        here = slice(block * BLOCK, (block + 1) * BLOCK)
        position = first + block * BLOCK + lax.broadcasted_iota(jnp.int32, (BLOCK, 1), 0)
        counts = jnp.minimum(position + 1, WINDOW).astype(F32)
        scale = 1.0 / (counts * ATT_DIM)
        for col in range(0, q_ref.shape[1], ATT_DIM):
            cols = slice(col, col + ATT_DIM)
            query = q_ref[here, cols]
            total = None
            for other in range(block - reach, block + 1):
                if other < 0:
                    there = slice((other + reach) * BLOCK, (other + reach + 1) * BLOCK)
                    key, value = prev_ref[0, there, cols], prev_ref[1, there, cols]
                else:
                    there = slice(other * BLOCK, (other + 1) * BLOCK)
                    key, value = k_ref[there, cols], v_ref[there, cols]
                score = jnp.maximum(outer_cols(query, key), 0.0)
                weight = score * score
                if other == block:
                    weight = jnp.where(col_at <= row_at, weight, 0.0)
                if other == block - reach:
                    weight = jnp.where(col_at > row_at, weight, 0.0)
                part = dot(weight.astype(BF16), value)
                total = part if total is None else total + part
            out_ref[here, cols] = total * scale
    for at, ref in enumerate((gate_ref, up_ref, down_ref)):
        whole = jnp.square(ref[...].astype(F32))
        square_ref[at] = jnp.sum(whole.reshape(-1, 8, whole.shape[1]), axis=0)


def apply_kernel(steps, part_rows, *refs):
    count = 2 * CHUNKS
    pieces, refs = refs[:count], refs[count:]
    q_ref, gate_ref, up_ref, down_ref, square_ref, attended_ref = refs[:6]
    combined_ref, sums_ref, next_gate_ref, next_up_ref, next_down_ref = refs[6:11]
    next_refs = refs[11:]
    bits = [bit_here(m) for m in steps]
    seq_index = lax.axis_index("seq")
    for at, (old_ref, new_ref) in enumerate(zip((gate_ref, up_ref, down_ref), next_refs)):
        size = old_ref.shape[0] * old_ref.shape[1]
        chunk_rows = old_ref.shape[0] // CHUNKS
        total = None
        for piece in pieces:
            part = jnp.square(piece[at].astype(F32))
            part = jnp.sum(part.reshape(-1, 8, part.shape[1]), axis=0)
            total = part if total is None else total + part
        grad_rms = jnp.sqrt(jnp.sum(total, keepdims=True) / size + EPSILON)
        weight_rms = jnp.sqrt(jnp.sum(square_ref[at], keepdims=True) / size)
        factor = ETA_STEP * weight_rms / grad_rms
        unit = chunk_rows >> len(steps)
        for chunk in range(CHUNKS):
            for arrived in range(2):
                piece = pieces[2 * chunk + arrived]
                for block in range(piece.shape[1] // unit):
                    start = chunk * chunk_rows
                    for p, bit in enumerate(bits):
                        came = arrived if p == 0 else (block >> (len(steps) - 1 - p)) & 1
                        start = start + (bit ^ came) * (chunk_rows >> (p + 1))
                    there = pl.ds(pl.multiple_of(start, unit), unit)
                    grad = piece[at, block * unit : (block + 1) * unit].astype(F32)
                    new_ref[there] = (old_ref[there].astype(F32) + factor * grad).astype(BF16)
    for new_ref, part_ref in zip(next_refs, (next_gate_ref, next_up_ref, next_down_ref)):
        kept = part_ref.shape[0]
        start = (seq_index * part_rows) // kept * kept
        part_ref[...] = new_ref[pl.ds(pl.multiple_of(start, kept), kept)]
    ones = jnp.ones((8, attended_ref.shape[1]), BF16)
    for block in range(q_ref.shape[0] // BLOCK):
        here = slice(block * BLOCK, (block + 1) * BLOCK)
        query = q_ref[here]
        gate_pre = dot(query, next_refs[0][...])
        up_pre = dot(query, next_refs[1][...])
        hidden = (gate_pre * jax.nn.sigmoid(gate_pre) * up_pre).astype(BF16)
        combined = attended_ref[here] + dot(hidden, next_refs[2][...])
        combined_ref[here] = combined
        squares = combined * combined
        high = squares.astype(BF16)
        low = (squares - high.astype(F32)).astype(BF16)
        sums_ref[:, here] = outer_cols(ones, high) + outer_cols(ones, low)


def norm_kernel(width, combined_ref, sums_ref, more_ref, gain_ref, out_ref):
    sums = sums_ref[...] if more_ref is None else sums_ref[...] + more_ref[...]
    scale = jnp.transpose(lax.rsqrt(sums / width + EPSILON))[:, :1]
    out_ref[...] = (combined_ref[...] * scale * gain_ref[...]).astype(BF16)


def body(queries, keys, values, rates, w_gate, w_up, w_down, out_gain):
    tok_rows, fw_dim = queries.shape
    seq_count, head_count = lax.axis_size("seq"), lax.axis_size("head")
    w_rows, w_cols = w_gate.shape
    weights = (w_gate, w_up, w_down)

    chunk_rows = w_rows // CHUNKS
    steps, others = exchange_masks(seq_count)
    half = chunk_rows // 2
    hbm = pl.BlockSpec(memory_space=pltpu.HBM)
    halves = [((3, half, w_cols), kind) for kind in (BF16, F32) for _ in range(CHUNKS)]
    key_tail, value_tail, *parts = pl.pallas_call(
        functools.partial(grads_kernel, steps[0]),
        out_shape=[jax.ShapeDtypeStruct((WINDOW, fw_dim), BF16)] * 2
        + [jax.ShapeDtypeStruct(*x) for x in halves],
        in_specs=[hbm] * 5 + [pl.BlockSpec(memory_space=pltpu.VMEM)],
        out_specs=[hbm] * (2 + len(halves)),
        name="gradients",
        scratch_shapes=[pltpu.VMEM(*x) for x in halves]
        + [
            pltpu.VMEM(keys.shape, BF16),
            pltpu.VMEM(values.shape, BF16),
            pltpu.VMEM(w_gate.shape, BF16),
            pltpu.VMEM(w_up.shape, BF16),
            pltpu.VMEM(w_down.shape, BF16),
            pltpu.VMEM(keys.shape, BF16),
            pltpu.VMEM((tok_rows, w_cols), BF16),
            pltpu.VMEM(values.shape, BF16),
            pltpu.VMEM((tok_rows, w_cols), BF16),
            pltpu.VMEM((tok_rows, w_cols), BF16),
            pltpu.SemaphoreType.DMA((5,)),
            pltpu.SemaphoreType.DMA((2,)),
            pltpu.SemaphoreType.DMA((3, len(halves))),
        ],
        compiler_params=pltpu.CompilerParams(vmem_limit_bytes=VMEM_WHOLE),
        cost_estimate=pl.CostEstimate(
            flops=12 * tok_rows * fw_dim * w_cols,
            bytes_accessed=16 * tok_rows * fw_dim,
            transcendentals=0,
        ),
    )(keys, values, *weights, rates.reshape(1, tok_rows))
    sent, kept = parts[:CHUNKS], parts[CHUNKS:]
    came = [swap(x, steps[0]) for x in sent]
    beside_k = trade(key_tail)
    folded = [fold(steps[1], [k], [c]) for k, c in zip(kept, came)]
    came = [swap(x, steps[1]) for x, _ in folded]
    came[0], beside_k = lax.optimization_barrier((came[0], beside_k))
    before_k = pass_on(beside_k)
    passed = pass_odd(value_tail)
    sent, kept = fold(steps[2], [k for _, k in folded], came)
    came = swap(sent, steps[2])
    total = kept + came.astype(F32)
    for masks in others:
        total = total.astype(BF16)
        came = swap(total, masks)
        total = total.astype(F32) + came.astype(F32)
    total = total.astype(BF16)
    more = swap(total, steps[2])
    rows = total.shape[1] // CHUNKS
    pieces = []
    for c in range(CHUNKS):
        here = slice(c * rows, (c + 1) * rows)
        piece = jnp.concatenate([total[:, here], more[:, here]], axis=1)
        came = swap(piece, steps[1])
        if c == 0:
            came, passed = lax.optimization_barrier((came, passed))
            prev_v = shift_passed(value_tail, passed)
        if c == 1:
            came, before_k = lax.optimization_barrier((came, before_k))
        piece = jnp.concatenate([piece, came], axis=1)
        pieces += [piece, swap(piece, steps[0])]

    attended, squares = pl.pallas_call(
        attend_kernel,
        out_shape=(
            jax.ShapeDtypeStruct((tok_rows, fw_dim), F32),
            jax.ShapeDtypeStruct((3, 8, w_cols), F32),
        ),
        in_specs=[pl.BlockSpec(memory_space=pltpu.VMEM)] * 3
        + [hbm] * 3
        + [pl.BlockSpec(memory_space=pltpu.VMEM)] * 3,
        name="window_attention",
        scratch_shapes=[pltpu.VMEM((2, WINDOW, fw_dim), BF16), pltpu.SemaphoreType.DMA((2,))],
        compiler_params=pltpu.CompilerParams(vmem_limit_bytes=VMEM_LIMIT),
        cost_estimate=pl.CostEstimate(
            flops=4 * tok_rows * (WINDOW + BLOCK) * fw_dim,
            bytes_accessed=8 * tok_rows * fw_dim,
            transcendentals=0,
        ),
    )(queries, keys, values, beside_k, before_k, prev_v, *weights)

    part_rows = w_rows // seq_count
    kept_rows = max(part_rows, SUBROWS)
    part_shape = jax.ShapeDtypeStruct((kept_rows, w_cols), BF16)
    combined, sums, *parts = pl.pallas_call(
        functools.partial(apply_kernel, steps, part_rows),
        out_shape=(
            jax.ShapeDtypeStruct((tok_rows, fw_dim), F32),
            jax.ShapeDtypeStruct((8, tok_rows), F32),
            part_shape,
            part_shape,
            part_shape,
        ),
        name="apply",
        scratch_shapes=[pltpu.VMEM((w_rows, w_cols), BF16)] * 3,
        compiler_params=pltpu.CompilerParams(vmem_limit_bytes=VMEM_LIMIT),
        cost_estimate=pl.CostEstimate(
            flops=6 * tok_rows * fw_dim * w_cols,
            bytes_accessed=12 * tok_rows * fw_dim,
            transcendentals=0,
        ),
    )(*pieces, queries, *weights, squares, attended)
    if part_rows < kept_rows:
        start = (lax.axis_index("seq") * part_rows) % kept_rows
        parts = [lax.dynamic_slice_in_dim(p, start, part_rows, 0) for p in parts]

    width = fw_dim * head_count
    if head_count == 2:
        more = [lax.ppermute(sums, "head", [(0, 1), (1, 0)])]
        norm = functools.partial(norm_kernel, width)
    else:
        sums, more = lax.psum(sums, "head"), []

        def norm(combined_ref, sums_ref, gain_ref, out_ref):
            norm_kernel(width, combined_ref, sums_ref, None, gain_ref, out_ref)

    output = kernel_call(
        norm,
        "norm",
        jax.ShapeDtypeStruct((tok_rows, fw_dim), BF16),
        4 * tok_rows * fw_dim,
        6 * tok_rows * fw_dim,
    )(combined, sums, *more, out_gain.reshape(1, fw_dim))
    return (output, *parts)


def solution(mesh):
    placed = (
        P("seq", "head"),
        P("seq", "head"),
        P("seq", "head"),
        P("seq", "head"),
        P("head", None),
        P("head", None),
        P("head", None),
        P("head"),
    )
    return jax.shard_map(
        body,
        mesh=mesh,
        in_specs=placed,
        out_specs=(
            P("seq", "head"),
            P(("head", "seq"), None),
            P(("head", "seq"), None),
            P(("head", "seq"), None),
        ),
        check_vma=False,
    )
```

```python
import functools

import jax
import jax.numpy as jnp
from jax import lax
from jax.experimental import pallas as pl
from jax.experimental.pallas import tpu as pltpu
from jax.sharding import PartitionSpec as P

ATT_DIM = 128
WINDOW = 512
BLOCK = 256
SUBROWS = 16
CHUNKS = 2


ETA_STEP = 0.5
EPSILON = 1e-06

F32 = jnp.float32
BF16 = jnp.bfloat16
VMEM_LIMIT = 40 * 1024 * 1024
VMEM_WHOLE = 62 * 1024 * 1024


def inner_rows(left_op, right_op):
    return lax.dot_general(
        left_op, right_op, (((0,), (0,)), ((), ())), preferred_element_type=F32
    )


def outer_cols(left_op, right_op):
    return lax.dot_general(
        left_op, right_op, (((1,), (1,)), ((), ())), preferred_element_type=F32
    )


def dot(left_op, right_op):
    return jnp.dot(left_op, right_op, preferred_element_type=F32)


def kernel_call(body, name, out_shape, flops, moved):
    return pl.pallas_call(
        body,
        out_shape=out_shape,
        name=name,
        compiler_params=pltpu.CompilerParams(vmem_limit_bytes=VMEM_LIMIT),
        cost_estimate=pl.CostEstimate(flops=flops, bytes_accessed=moved, transcendentals=0),
    )


def exchange_masks(peers):
    bits = [1 << at for at in range(peers.bit_length() - 1)]
    halving = [(bits[2], bits[1]), (bits[1], bits[2]), (bits[0], bits[0])]
    return halving, [(b, b) for b in bits[3:]]


def mask_here(masks):
    return jnp.where(lax.axis_index("head") % 2 == 0, masks[0], masks[1])


def bit_here(masks):
    return ((lax.axis_index("seq") & mask_here(masks)) != 0).astype(jnp.int32)


def swap(x, masks):
    peers, heads = lax.axis_size("seq"), lax.axis_size("head")
    pairs = [
        (s * heads + h, (s ^ masks[h % 2]) * heads + h)
        for s in range(peers)
        for h in range(heads)
    ]
    return lax.ppermute(x, ("seq", "head"), pairs)


def pass_odd(x):
    return lax.ppermute(x, "seq", [(i, i + 2) for i in range(1, lax.axis_size("seq") - 2, 2)])


def shift_passed(x, passed):
    peers = lax.axis_size("seq")
    odd = lax.axis_index("seq") % 2 == 1
    pairs = [(i, i + 1) for i in range(0, peers, 2)] + [(i, i - 1) for i in range(1, peers, 2)]
    return lax.ppermute(jnp.where(odd, passed, x), "seq", pairs)


def trade(x):
    peers = lax.axis_size("seq")
    return lax.ppermute(x, "seq", [(i, i ^ 1) for i in range(peers)])


def pass_on(x):
    return lax.ppermute(x, "seq", [(i, i + 2) for i in range(0, lax.axis_size("seq") - 2, 2)])


def grads_kernel(step, *refs):
    k_hbm, v_hbm, gate_hbm, up_hbm, down_hbm, rate_ref, *tail_hbms = refs[:8]
    outs = refs[8 : 8 + 2 * CHUNKS]
    refs = refs[8 + 2 * CHUNKS :]
    held, refs = refs[: 2 * CHUNKS], refs[2 * CHUNKS :]
    k_ref, v_ref, gate_ref, up_ref, down_ref, order_ref, hidden_ref, target_ref, d_gate_ref, d_up_ref = refs[:10]
    in_sems, tail_sems, out_sems = refs[10:]
    moves = ((k_hbm, k_ref), (gate_hbm, gate_ref), (up_hbm, up_ref), (v_hbm, v_ref), (down_hbm, down_ref))
    copies = [pltpu.make_async_copy(a, b, in_sems.at[at]) for at, (a, b) in enumerate(moves)]
    for copy in copies:
        copy.start()
    rows = k_ref.shape[0]
    half = held[0].shape[1]
    bit = bit_here(step)
    places = []
    for chunk in range(CHUNKS):
        for to in (1 - bit, bit):
            places.append(pl.ds(pl.multiple_of((2 * chunk + to) * half, half), half))
    tail = pl.ds(rows - WINDOW, WINDOW)
    tails = [
        pltpu.make_async_copy(ref.at[tail], tail_hbms[at], tail_sems.at[at])
        for at, ref in enumerate((k_ref, v_ref))
    ]
    copies[0].wait()
    tails[0].start()
    for at, place in enumerate(places):
        order_ref[:, place] = k_ref[:, at * half : (at + 1) * half]
    rate_col = jnp.transpose(jnp.broadcast_to(rate_ref[...], (8, rows)))[:, :1]
    for copy in copies[1:]:
        copy.wait()
    tails[1].start()
    for start in range(0, rows, BLOCK):
        here = slice(start, start + BLOCK)
        gate_pre = dot(k_ref[here], gate_ref[...])
        up_pre = dot(k_ref[here], up_ref[...])
        target = (rate_col[here] * v_ref[here].astype(F32)).astype(BF16)
        target_ref[here] = target
        backward = outer_cols(target, down_ref[...])
        sigmoid_val = jax.nn.sigmoid(gate_pre)
        activated = gate_pre * sigmoid_val
        hidden = (activated * up_pre).astype(BF16)
        for at, place in enumerate(places):
            hidden_ref[here, place] = hidden[:, at * half : (at + 1) * half]
        d_up_ref[here] = (backward * activated).astype(BF16)
        derivative = sigmoid_val * (1.0 + gate_pre * (1.0 - sigmoid_val))
        d_gate_ref[here] = (backward * up_pre * derivative).astype(BF16)
    results = []
    for matrix, (left, right) in enumerate(
        ((order_ref, d_gate_ref), (order_ref, d_up_ref), (hidden_ref, target_ref))
    ):
        product = inner_rows(left[...], right[...])
        for chunk in range(CHUNKS):
            start = 2 * chunk * half
            held[chunk][matrix] = product[start : start + half].astype(BF16)
            held[CHUNKS + chunk][matrix] = product[start + half : start + 2 * half]
        for at in range(2 * CHUNKS):
            copy = pltpu.make_async_copy(held[at].at[matrix], outs[at].at[matrix], out_sems.at[matrix, at])
            copy.start()
            results.append(copy)
    for copy in tails + results:
        copy.wait()


def fold_kernel(step, *refs):
    sent_ref, next_ref = refs[-2:]
    kept_refs, came_refs = refs[: len(refs) // 2 - 1], refs[len(refs) // 2 - 1 : -2]
    half = sent_ref.shape[1] // len(kept_refs)
    bit = bit_here(step)
    for at, (kept_ref, came_ref) in enumerate(zip(kept_refs, came_refs)):
        there = slice(at * half, (at + 1) * half)
        for which, ref in ((1 - bit, sent_ref), (bit, next_ref)):
            rows = pl.ds(pl.multiple_of(which * half, half), half)
            ref[:, there] = (kept_ref[:, rows] + came_ref[:, rows].astype(F32)).astype(ref.dtype)


def fold(step, kept, came):
    rows = sum(k.shape[1] // 2 for k in kept)
    shape = (kept[0].shape[0], rows, kept[0].shape[2])
    size = shape[0] * shape[1] * shape[2]
    return kernel_call(
        functools.partial(fold_kernel, step),
        "fold",
        (jax.ShapeDtypeStruct(shape, BF16), jax.ShapeDtypeStruct(shape, F32)),
        2 * size,
        18 * size,
    )(*kept, *came)


def attend_kernel(
    q_ref, k_ref, v_ref, odd_k, even_k, prev_v, gate_ref, up_ref, down_ref, out_ref, square_ref, prev_ref, sems
):
    rows = q_ref.shape[0]
    odd = lax.axis_index("seq") % 2 == 1
    value_copy = pltpu.make_async_copy(prev_v, prev_ref.at[1], sems.at[1])
    value_copy.start()

    @pl.when(odd)
    def _():
        pltpu.make_async_copy(odd_k, prev_ref.at[0], sems.at[0]).start()

    @pl.when(jnp.logical_not(odd))
    def _():
        pltpu.make_async_copy(even_k, prev_ref.at[0], sems.at[0]).start()

    pltpu.make_async_copy(even_k, prev_ref.at[0], sems.at[0]).wait()
    value_copy.wait()
    reach = WINDOW // BLOCK
    row_at = lax.broadcasted_iota(jnp.int32, (BLOCK, BLOCK), 0)
    col_at = lax.broadcasted_iota(jnp.int32, (BLOCK, BLOCK), 1)
    first = lax.axis_index("seq") * rows
    for block in range(rows // BLOCK):
        here = slice(block * BLOCK, (block + 1) * BLOCK)
        position = first + block * BLOCK + lax.broadcasted_iota(jnp.int32, (BLOCK, 1), 0)
        counts = jnp.minimum(position + 1, WINDOW).astype(F32)
        scale = 1.0 / (counts * ATT_DIM)
        for col in range(0, q_ref.shape[1], ATT_DIM):
            cols = slice(col, col + ATT_DIM)
            query = q_ref[here, cols]
            total = None
            for other in range(block - reach, block + 1):
                if other < 0:
                    there = slice((other + reach) * BLOCK, (other + reach + 1) * BLOCK)
                    key, value = prev_ref[0, there, cols], prev_ref[1, there, cols]
                else:
                    there = slice(other * BLOCK, (other + 1) * BLOCK)
                    key, value = k_ref[there, cols], v_ref[there, cols]
                score = jnp.maximum(outer_cols(query, key), 0.0)
                weight = score * score
                if other == block:
                    weight = jnp.where(col_at <= row_at, weight, 0.0)
                if other == block - reach:
                    weight = jnp.where(col_at > row_at, weight, 0.0)
                part = dot(weight.astype(BF16), value)
                total = part if total is None else total + part
            out_ref[here, cols] = total * scale
    for at, ref in enumerate((gate_ref, up_ref, down_ref)):
        whole = jnp.square(ref[...].astype(F32))
        square_ref[at] = jnp.sum(whole.reshape(-1, 8, whole.shape[1]), axis=0)


def apply_kernel(steps, part_rows, *refs):
    count = 2 * CHUNKS
    pieces, refs = refs[:count], refs[count:]
    q_ref, gate_ref, up_ref, down_ref, square_ref, attended_ref = refs[:6]
    combined_ref, sums_ref, next_gate_ref, next_up_ref, next_down_ref = refs[6:11]
    next_refs = refs[11:]
    bits = [bit_here(m) for m in steps]
    seq_index = lax.axis_index("seq")
    blocks = [slice(start, start + BLOCK) for start in range(0, q_ref.shape[0], BLOCK)]
    ahead = []
    for at, (old_ref, new_ref) in enumerate(zip((gate_ref, up_ref, down_ref), next_refs)):
        size = old_ref.shape[0] * old_ref.shape[1]
        chunk_rows = old_ref.shape[0] // CHUNKS
        total = None
        for piece in pieces:
            part = jnp.square(piece[at].astype(F32))
            part = jnp.sum(part.reshape(-1, 8, part.shape[1]), axis=0)
            total = part if total is None else total + part
        grad_rms = jnp.sqrt(jnp.sum(total, keepdims=True) / size + EPSILON)
        weight_rms = jnp.sqrt(jnp.sum(square_ref[at], keepdims=True) / size)
        factor = ETA_STEP * weight_rms / grad_rms
        unit = chunk_rows >> len(steps)
        for chunk in range(CHUNKS):
            for arrived in range(2):
                piece = pieces[2 * chunk + arrived]
                for block in range(piece.shape[1] // unit):
                    start = chunk * chunk_rows
                    for p, bit in enumerate(bits):
                        came = arrived if p == 0 else (block >> (len(steps) - 1 - p)) & 1
                        start = start + (bit ^ came) * (chunk_rows >> (p + 1))
                    there = pl.ds(pl.multiple_of(start, unit), unit)
                    grad = piece[at, block * unit : (block + 1) * unit].astype(F32)
                    new_ref[there] = (old_ref[there].astype(F32) + factor * grad).astype(BF16)
        if at < 2:
            ahead.append([dot(q_ref[here], new_ref[...]) for here in blocks])
    for new_ref, part_ref in zip(next_refs, (next_gate_ref, next_up_ref, next_down_ref)):
        kept = part_ref.shape[0]
        start = (seq_index * part_rows) // kept * kept
        part_ref[...] = new_ref[pl.ds(pl.multiple_of(start, kept), kept)]
    ones = jnp.ones((8, attended_ref.shape[1]), BF16)
    for here, gate_pre, up_pre in zip(blocks, *ahead):
        hidden = (gate_pre * jax.nn.sigmoid(gate_pre) * up_pre).astype(BF16)
        combined = attended_ref[here] + dot(hidden, next_refs[2][...])
        combined_ref[here] = combined
        squares = combined * combined
        high = squares.astype(BF16)
        low = (squares - high.astype(F32)).astype(BF16)
        sums_ref[:, here] = outer_cols(ones, high) + outer_cols(ones, low)


def norm_kernel(width, combined_ref, sums_ref, more_ref, gain_ref, out_ref):
    sums = sums_ref[...] if more_ref is None else sums_ref[...] + more_ref[...]
    scale = jnp.transpose(lax.rsqrt(sums / width + EPSILON))[:, :1]
    out_ref[...] = (combined_ref[...] * scale * gain_ref[...]).astype(BF16)


def body(queries, keys, values, rates, w_gate, w_up, w_down, out_gain):
    tok_rows, fw_dim = queries.shape
    seq_count, head_count = lax.axis_size("seq"), lax.axis_size("head")
    w_rows, w_cols = w_gate.shape
    weights = (w_gate, w_up, w_down)

    chunk_rows = w_rows // CHUNKS
    steps, others = exchange_masks(seq_count)
    half = chunk_rows // 2
    hbm = pl.BlockSpec(memory_space=pltpu.HBM)
    halves = [((3, half, w_cols), kind) for kind in (BF16, F32) for _ in range(CHUNKS)]
    key_tail, value_tail, *parts = pl.pallas_call(
        functools.partial(grads_kernel, steps[0]),
        out_shape=[jax.ShapeDtypeStruct((WINDOW, fw_dim), BF16)] * 2
        + [jax.ShapeDtypeStruct(*x) for x in halves],
        in_specs=[hbm] * 5 + [pl.BlockSpec(memory_space=pltpu.VMEM)],
        out_specs=[hbm] * (2 + len(halves)),
        name="gradients",
        scratch_shapes=[pltpu.VMEM(*x) for x in halves]
        + [
            pltpu.VMEM(keys.shape, BF16),
            pltpu.VMEM(values.shape, BF16),
            pltpu.VMEM(w_gate.shape, BF16),
            pltpu.VMEM(w_up.shape, BF16),
            pltpu.VMEM(w_down.shape, BF16),
            pltpu.VMEM(keys.shape, BF16),
            pltpu.VMEM((tok_rows, w_cols), BF16),
            pltpu.VMEM(values.shape, BF16),
            pltpu.VMEM((tok_rows, w_cols), BF16),
            pltpu.VMEM((tok_rows, w_cols), BF16),
            pltpu.SemaphoreType.DMA((5,)),
            pltpu.SemaphoreType.DMA((2,)),
            pltpu.SemaphoreType.DMA((3, len(halves))),
        ],
        compiler_params=pltpu.CompilerParams(vmem_limit_bytes=VMEM_WHOLE),
        cost_estimate=pl.CostEstimate(
            flops=12 * tok_rows * fw_dim * w_cols,
            bytes_accessed=16 * tok_rows * fw_dim,
            transcendentals=0,
        ),
    )(keys, values, *weights, rates.reshape(1, tok_rows))
    sent, kept = parts[:CHUNKS], parts[CHUNKS:]
    came = [swap(x, steps[0]) for x in sent]
    beside_k = trade(key_tail)
    folded = [fold(steps[1], [k], [c]) for k, c in zip(kept, came)]
    came = [swap(x, steps[1]) for x, _ in folded]
    came[0], beside_k = lax.optimization_barrier((came[0], beside_k))
    before_k = pass_on(beside_k)
    passed = pass_odd(value_tail)
    sent, kept = fold(steps[2], [k for _, k in folded], came)
    came = swap(sent, steps[2])
    total = kept + came.astype(F32)
    for masks in others:
        total = total.astype(BF16)
        came = swap(total, masks)
        total = total.astype(F32) + came.astype(F32)
    total = total.astype(BF16)
    more = swap(total, steps[2])
    rows = total.shape[1] // CHUNKS
    pieces = []
    for c in range(CHUNKS):
        here = slice(c * rows, (c + 1) * rows)
        piece = jnp.concatenate([total[:, here], more[:, here]], axis=1)
        came = swap(piece, steps[1])
        if c == 0:
            came, passed = lax.optimization_barrier((came, passed))
            prev_v = shift_passed(value_tail, passed)
        if c == 1:
            came, before_k = lax.optimization_barrier((came, before_k))
        piece = jnp.concatenate([piece, came], axis=1)
        pieces += [piece, swap(piece, steps[0])]

    attended, squares = pl.pallas_call(
        attend_kernel,
        out_shape=(
            jax.ShapeDtypeStruct((tok_rows, fw_dim), F32),
            jax.ShapeDtypeStruct((3, 8, w_cols), F32),
        ),
        in_specs=[pl.BlockSpec(memory_space=pltpu.VMEM)] * 3
        + [hbm] * 3
        + [pl.BlockSpec(memory_space=pltpu.VMEM)] * 3,
        name="window_attention",
        scratch_shapes=[pltpu.VMEM((2, WINDOW, fw_dim), BF16), pltpu.SemaphoreType.DMA((2,))],
        compiler_params=pltpu.CompilerParams(vmem_limit_bytes=VMEM_LIMIT),
        cost_estimate=pl.CostEstimate(
            flops=4 * tok_rows * (WINDOW + BLOCK) * fw_dim,
            bytes_accessed=8 * tok_rows * fw_dim,
            transcendentals=0,
        ),
    )(queries, keys, values, beside_k, before_k, prev_v, *weights)

    part_rows = w_rows // seq_count
    kept_rows = max(part_rows, SUBROWS)
    part_shape = jax.ShapeDtypeStruct((kept_rows, w_cols), BF16)
    combined, sums, *parts = pl.pallas_call(
        functools.partial(apply_kernel, steps, part_rows),
        out_shape=(
            jax.ShapeDtypeStruct((tok_rows, fw_dim), F32),
            jax.ShapeDtypeStruct((8, tok_rows), F32),
            part_shape,
            part_shape,
            part_shape,
        ),
        name="apply",
        scratch_shapes=[pltpu.VMEM((w_rows, w_cols), BF16)] * 3,
        compiler_params=pltpu.CompilerParams(vmem_limit_bytes=VMEM_LIMIT),
        cost_estimate=pl.CostEstimate(
            flops=6 * tok_rows * fw_dim * w_cols,
            bytes_accessed=12 * tok_rows * fw_dim,
            transcendentals=0,
        ),
    )(*pieces, queries, *weights, squares, attended)
    if part_rows < kept_rows:
        start = (lax.axis_index("seq") * part_rows) % kept_rows
        parts = [lax.dynamic_slice_in_dim(p, start, part_rows, 0) for p in parts]

    width = fw_dim * head_count
    if head_count == 2:
        more = [lax.ppermute(sums, "head", [(0, 1), (1, 0)])]
        norm = functools.partial(norm_kernel, width)
    else:
        sums, more = lax.psum(sums, "head"), []

        def norm(combined_ref, sums_ref, gain_ref, out_ref):
            norm_kernel(width, combined_ref, sums_ref, None, gain_ref, out_ref)

    output = kernel_call(
        norm,
        "norm",
        jax.ShapeDtypeStruct((tok_rows, fw_dim), BF16),
        4 * tok_rows * fw_dim,
        6 * tok_rows * fw_dim,
    )(combined, sums, *more, out_gain.reshape(1, fw_dim))
    return (output, *parts)


def solution(mesh):
    placed = (
        P("seq", "head"),
        P("seq", "head"),
        P("seq", "head"),
        P("seq", "head"),
        P("head", None),
        P("head", None),
        P("head", None),
        P("head"),
    )
    return jax.shard_map(
        body,
        mesh=mesh,
        in_specs=placed,
        out_specs=(
            P("seq", "head"),
            P(("head", "seq"), None),
            P(("head", "seq"), None),
            P(("head", "seq"), None),
        ),
        check_vma=False,
    )
```

```python
import functools

import jax
import jax.numpy as jnp
from jax import lax
from jax.experimental import pallas as pl
from jax.experimental.pallas import tpu as pltpu
from jax.sharding import PartitionSpec as P

ATT_DIM = 128
WINDOW = 512
BLOCK = 256
SUBROWS = 16
CHUNKS = 2


ETA_STEP = 0.5
EPSILON = 1e-06

F32 = jnp.float32
BF16 = jnp.bfloat16
VMEM_LIMIT = 40 * 1024 * 1024
VMEM_WHOLE = 62 * 1024 * 1024


def inner_rows(left_op, right_op):
    return lax.dot_general(
        left_op, right_op, (((0,), (0,)), ((), ())), preferred_element_type=F32
    )


def outer_cols(left_op, right_op):
    return lax.dot_general(
        left_op, right_op, (((1,), (1,)), ((), ())), preferred_element_type=F32
    )


def dot(left_op, right_op):
    return jnp.dot(left_op, right_op, preferred_element_type=F32)


def kernel_call(body, name, out_shape, flops, moved):
    return pl.pallas_call(
        body,
        out_shape=out_shape,
        name=name,
        compiler_params=pltpu.CompilerParams(vmem_limit_bytes=VMEM_LIMIT),
        cost_estimate=pl.CostEstimate(flops=flops, bytes_accessed=moved, transcendentals=0),
    )


def exchange_masks(peers):
    bits = [1 << at for at in range(peers.bit_length() - 1)]
    halving = [(bits[2], bits[1]), (bits[1], bits[2]), (bits[0], bits[0])]
    return halving, [(b, b) for b in bits[3:]]


def mask_here(masks):
    return jnp.where(lax.axis_index("head") % 2 == 0, masks[0], masks[1])


def bit_here(masks):
    return ((lax.axis_index("seq") & mask_here(masks)) != 0).astype(jnp.int32)


def swap(x, masks):
    peers, heads = lax.axis_size("seq"), lax.axis_size("head")
    pairs = [
        (s * heads + h, (s ^ masks[h % 2]) * heads + h)
        for s in range(peers)
        for h in range(heads)
    ]
    return lax.ppermute(x, ("seq", "head"), pairs)


def pass_odd(x):
    return lax.ppermute(x, "seq", [(i, i + 2) for i in range(1, lax.axis_size("seq") - 2, 2)])


def shift_passed(x, passed):
    peers = lax.axis_size("seq")
    odd = lax.axis_index("seq") % 2 == 1
    pairs = [(i, i + 1) for i in range(0, peers, 2)] + [(i, i - 1) for i in range(1, peers, 2)]
    return lax.ppermute(jnp.where(odd, passed, x), "seq", pairs)


def trade(x):
    peers = lax.axis_size("seq")
    return lax.ppermute(x, "seq", [(i, i ^ 1) for i in range(peers)])


def pass_on(x):
    return lax.ppermute(x, "seq", [(i, i + 2) for i in range(0, lax.axis_size("seq") - 2, 2)])


def grads_kernel(step, *refs):
    k_hbm, v_hbm, gate_hbm, up_hbm, down_hbm, rate_ref, *tail_hbms = refs[:8]
    outs = refs[8 : 8 + 2 * CHUNKS]
    refs = refs[8 + 2 * CHUNKS :]
    held, refs = refs[: 2 * CHUNKS], refs[2 * CHUNKS :]
    k_ref, v_ref, gate_ref, up_ref, down_ref, order_ref, hidden_ref, target_ref, d_gate_ref, d_up_ref = refs[:10]
    in_sems, tail_sems, out_sems = refs[10:]
    moves = ((k_hbm, k_ref), (gate_hbm, gate_ref), (up_hbm, up_ref), (v_hbm, v_ref), (down_hbm, down_ref))
    copies = [pltpu.make_async_copy(a, b, in_sems.at[at]) for at, (a, b) in enumerate(moves)]
    for copy in copies:
        copy.start()
    rows = k_ref.shape[0]
    half = held[0].shape[1]
    bit = bit_here(step)
    places = []
    for chunk in range(CHUNKS):
        for to in (1 - bit, bit):
            places.append(pl.ds(pl.multiple_of((2 * chunk + to) * half, half), half))
    tail = pl.ds(rows - WINDOW, WINDOW)
    tails = [
        pltpu.make_async_copy(ref.at[tail], tail_hbms[at], tail_sems.at[at])
        for at, ref in enumerate((k_ref, v_ref))
    ]
    copies[0].wait()
    tails[0].start()
    for at, place in enumerate(places):
        order_ref[:, place] = k_ref[:, at * half : (at + 1) * half]
    rate_col = jnp.transpose(jnp.broadcast_to(rate_ref[...], (8, rows)))[:, :1]
    for start in range(0, rows, BLOCK):
        here = slice(start, start + BLOCK)
        if start == 0:
            copies[1].wait()
        gate_pre = dot(k_ref[here], gate_ref[...])
        if start == 0:
            copies[2].wait()
        up_pre = dot(k_ref[here], up_ref[...])
        if start == 0:
            copies[3].wait()
            copies[4].wait()
            tails[1].start()
        target = (rate_col[here] * v_ref[here].astype(F32)).astype(BF16)
        target_ref[here] = target
        backward = outer_cols(target, down_ref[...])
        sigmoid_val = jax.nn.sigmoid(gate_pre)
        activated = gate_pre * sigmoid_val
        hidden = (activated * up_pre).astype(BF16)
        for at, place in enumerate(places):
            hidden_ref[here, place] = hidden[:, at * half : (at + 1) * half]
        d_up_ref[here] = (backward * activated).astype(BF16)
        derivative = sigmoid_val * (1.0 + gate_pre * (1.0 - sigmoid_val))
        d_gate_ref[here] = (backward * up_pre * derivative).astype(BF16)
    results = []
    for matrix, (left, right) in enumerate(
        ((order_ref, d_gate_ref), (order_ref, d_up_ref), (hidden_ref, target_ref))
    ):
        product = inner_rows(left[...], right[...])
        for chunk in range(CHUNKS):
            start = 2 * chunk * half
            held[chunk][matrix] = product[start : start + half].astype(BF16)
            held[CHUNKS + chunk][matrix] = product[start + half : start + 2 * half]
        for at in range(2 * CHUNKS):
            copy = pltpu.make_async_copy(held[at].at[matrix], outs[at].at[matrix], out_sems.at[matrix, at])
            copy.start()
            results.append(copy)
    for copy in tails + results:
        copy.wait()


def fold_kernel(step, *refs):
    sent_ref, next_ref = refs[-2:]
    kept_refs, came_refs = refs[: len(refs) // 2 - 1], refs[len(refs) // 2 - 1 : -2]
    half = sent_ref.shape[1] // len(kept_refs)
    bit = bit_here(step)
    for at, (kept_ref, came_ref) in enumerate(zip(kept_refs, came_refs)):
        there = slice(at * half, (at + 1) * half)
        for which, ref in ((1 - bit, sent_ref), (bit, next_ref)):
            rows = pl.ds(pl.multiple_of(which * half, half), half)
            ref[:, there] = (kept_ref[:, rows] + came_ref[:, rows].astype(F32)).astype(ref.dtype)


def fold(step, kept, came):
    rows = sum(k.shape[1] // 2 for k in kept)
    shape = (kept[0].shape[0], rows, kept[0].shape[2])
    size = shape[0] * shape[1] * shape[2]
    return kernel_call(
        functools.partial(fold_kernel, step),
        "fold",
        (jax.ShapeDtypeStruct(shape, BF16), jax.ShapeDtypeStruct(shape, F32)),
        2 * size,
        18 * size,
    )(*kept, *came)


def attend_kernel(
    q_ref, k_ref, v_ref, odd_k, even_k, prev_v, gate_ref, up_ref, down_ref, out_ref, square_ref, prev_ref, sems
):
    rows = q_ref.shape[0]
    odd = lax.axis_index("seq") % 2 == 1
    value_copy = pltpu.make_async_copy(prev_v, prev_ref.at[1], sems.at[1])
    value_copy.start()

    @pl.when(odd)
    def _():
        pltpu.make_async_copy(odd_k, prev_ref.at[0], sems.at[0]).start()

    @pl.when(jnp.logical_not(odd))
    def _():
        pltpu.make_async_copy(even_k, prev_ref.at[0], sems.at[0]).start()

    pltpu.make_async_copy(even_k, prev_ref.at[0], sems.at[0]).wait()
    value_copy.wait()
    reach = WINDOW // BLOCK
    row_at = lax.broadcasted_iota(jnp.int32, (BLOCK, BLOCK), 0)
    col_at = lax.broadcasted_iota(jnp.int32, (BLOCK, BLOCK), 1)
    first = lax.axis_index("seq") * rows
    for block in range(rows // BLOCK):
        here = slice(block * BLOCK, (block + 1) * BLOCK)
        position = first + block * BLOCK + lax.broadcasted_iota(jnp.int32, (BLOCK, 1), 0)
        counts = jnp.minimum(position + 1, WINDOW).astype(F32)
        scale = 1.0 / (counts * ATT_DIM)
        for col in range(0, q_ref.shape[1], ATT_DIM):
            cols = slice(col, col + ATT_DIM)
            query = q_ref[here, cols]
            total = None
            for other in range(block - reach, block + 1):
                if other < 0:
                    there = slice((other + reach) * BLOCK, (other + reach + 1) * BLOCK)
                    key, value = prev_ref[0, there, cols], prev_ref[1, there, cols]
                else:
                    there = slice(other * BLOCK, (other + 1) * BLOCK)
                    key, value = k_ref[there, cols], v_ref[there, cols]
                score = jnp.maximum(outer_cols(query, key), 0.0)
                weight = score * score
                if other == block:
                    weight = jnp.where(col_at <= row_at, weight, 0.0)
                if other == block - reach:
                    weight = jnp.where(col_at > row_at, weight, 0.0)
                part = dot(weight.astype(BF16), value)
                total = part if total is None else total + part
            out_ref[here, cols] = total * scale
    for at, ref in enumerate((gate_ref, up_ref, down_ref)):
        whole = jnp.square(ref[...].astype(F32))
        square_ref[at] = jnp.sum(whole.reshape(-1, 8, whole.shape[1]), axis=0)


def apply_kernel(steps, part_rows, *refs):
    count = 2 * CHUNKS
    pieces, refs = refs[:count], refs[count:]
    q_ref, gate_ref, up_ref, down_ref, square_ref, attended_ref = refs[:6]
    combined_ref, sums_ref, next_gate_ref, next_up_ref, next_down_ref = refs[6:11]
    next_refs = refs[11:]
    bits = [bit_here(m) for m in steps]
    seq_index = lax.axis_index("seq")
    blocks = [slice(start, start + BLOCK) for start in range(0, q_ref.shape[0], BLOCK)]
    ahead = []
    for at, (old_ref, new_ref) in enumerate(zip((gate_ref, up_ref, down_ref), next_refs)):
        size = old_ref.shape[0] * old_ref.shape[1]
        chunk_rows = old_ref.shape[0] // CHUNKS
        total = None
        for piece in pieces:
            part = jnp.square(piece[at].astype(F32))
            part = jnp.sum(part.reshape(-1, 8, part.shape[1]), axis=0)
            total = part if total is None else total + part
        grad_rms = jnp.sqrt(jnp.sum(total, keepdims=True) / size + EPSILON)
        weight_rms = jnp.sqrt(jnp.sum(square_ref[at], keepdims=True) / size)
        factor = ETA_STEP * weight_rms / grad_rms
        unit = chunk_rows >> len(steps)
        for chunk in range(CHUNKS):
            for arrived in range(2):
                piece = pieces[2 * chunk + arrived]
                for block in range(piece.shape[1] // unit):
                    start = chunk * chunk_rows
                    for p, bit in enumerate(bits):
                        came = arrived if p == 0 else (block >> (len(steps) - 1 - p)) & 1
                        start = start + (bit ^ came) * (chunk_rows >> (p + 1))
                    there = pl.ds(pl.multiple_of(start, unit), unit)
                    grad = piece[at, block * unit : (block + 1) * unit].astype(F32)
                    new_ref[there] = (old_ref[there].astype(F32) + factor * grad).astype(BF16)
        if at < 2:
            ahead.append([dot(q_ref[here], new_ref[...]) for here in blocks])
    for new_ref, part_ref in zip(next_refs, (next_gate_ref, next_up_ref, next_down_ref)):
        kept = part_ref.shape[0]
        start = (seq_index * part_rows) // kept * kept
        part_ref[...] = new_ref[pl.ds(pl.multiple_of(start, kept), kept)]
    ones = jnp.ones((8, attended_ref.shape[1]), BF16)
    for here, gate_pre, up_pre in zip(blocks, *ahead):
        hidden = (gate_pre * jax.nn.sigmoid(gate_pre) * up_pre).astype(BF16)
        combined = attended_ref[here] + dot(hidden, next_refs[2][...])
        combined_ref[here] = combined
        squares = combined * combined
        high = squares.astype(BF16)
        low = (squares - high.astype(F32)).astype(BF16)
        sums_ref[:, here] = outer_cols(ones, high) + outer_cols(ones, low)


def norm_kernel(width, combined_ref, *refs):
    *sums_refs, gain_ref, out_hbm, held_ref, sems = refs
    sums = sums_refs[0][...]
    for ref in sums_refs[1:]:
        sums = sums + ref[...]
    scale = jnp.transpose(lax.rsqrt(sums / width + EPSILON))[:, :1]
    copies = []
    for at, start in enumerate(range(0, held_ref.shape[0], BLOCK // 2)):
        here = slice(start, start + BLOCK // 2)
        held_ref[here] = (combined_ref[here] * scale[here] * gain_ref[...]).astype(BF16)
        copies.append(pltpu.make_async_copy(held_ref.at[here], out_hbm.at[here], sems.at[at]))
        copies[-1].start()
    for copy in copies:
        copy.wait()


def body(queries, keys, values, rates, w_gate, w_up, w_down, out_gain):
    tok_rows, fw_dim = queries.shape
    seq_count, head_count = lax.axis_size("seq"), lax.axis_size("head")
    w_rows, w_cols = w_gate.shape
    weights = (w_gate, w_up, w_down)

    chunk_rows = w_rows // CHUNKS
    steps, others = exchange_masks(seq_count)
    half = chunk_rows // 2
    hbm = pl.BlockSpec(memory_space=pltpu.HBM)
    halves = [((3, half, w_cols), kind) for kind in (BF16, F32) for _ in range(CHUNKS)]
    key_tail, value_tail, *parts = pl.pallas_call(
        functools.partial(grads_kernel, steps[0]),
        out_shape=[jax.ShapeDtypeStruct((WINDOW, fw_dim), BF16)] * 2
        + [jax.ShapeDtypeStruct(*x) for x in halves],
        in_specs=[hbm] * 5 + [pl.BlockSpec(memory_space=pltpu.VMEM)],
        out_specs=[hbm] * (2 + len(halves)),
        name="gradients",
        scratch_shapes=[pltpu.VMEM(*x) for x in halves]
        + [
            pltpu.VMEM(keys.shape, BF16),
            pltpu.VMEM(values.shape, BF16),
            pltpu.VMEM(w_gate.shape, BF16),
            pltpu.VMEM(w_up.shape, BF16),
            pltpu.VMEM(w_down.shape, BF16),
            pltpu.VMEM(keys.shape, BF16),
            pltpu.VMEM((tok_rows, w_cols), BF16),
            pltpu.VMEM(values.shape, BF16),
            pltpu.VMEM((tok_rows, w_cols), BF16),
            pltpu.VMEM((tok_rows, w_cols), BF16),
            pltpu.SemaphoreType.DMA((5,)),
            pltpu.SemaphoreType.DMA((2,)),
            pltpu.SemaphoreType.DMA((3, len(halves))),
        ],
        compiler_params=pltpu.CompilerParams(vmem_limit_bytes=VMEM_WHOLE),
        cost_estimate=pl.CostEstimate(
            flops=12 * tok_rows * fw_dim * w_cols,
            bytes_accessed=16 * tok_rows * fw_dim,
            transcendentals=0,
        ),
    )(keys, values, *weights, rates.reshape(1, tok_rows))
    sent, kept = parts[:CHUNKS], parts[CHUNKS:]
    came = [swap(x, steps[0]) for x in sent]
    beside_k = trade(key_tail)
    folded = [fold(steps[1], [k], [c]) for k, c in zip(kept, came)]
    came = [swap(x, steps[1]) for x, _ in folded]
    came[0], beside_k = lax.optimization_barrier((came[0], beside_k))
    before_k = pass_on(beside_k)
    passed = pass_odd(value_tail)
    sent, kept = fold(steps[2], [k for _, k in folded], came)
    came = swap(sent, steps[2])
    total = kept + came.astype(F32)
    for masks in others:
        total = total.astype(BF16)
        came = swap(total, masks)
        total = total.astype(F32) + came.astype(F32)
    total = total.astype(BF16)
    more = swap(total, steps[2])
    rows = total.shape[1] // CHUNKS
    pieces = []
    for c in range(CHUNKS):
        here = slice(c * rows, (c + 1) * rows)
        piece = jnp.concatenate([total[:, here], more[:, here]], axis=1)
        came = swap(piece, steps[1])
        if c == 1:
            came, passed, before_k = lax.optimization_barrier((came, passed, before_k))
            prev_v = shift_passed(value_tail, passed)
        piece = jnp.concatenate([piece, came], axis=1)
        pieces += [piece, swap(piece, steps[0])]

    attended, squares = pl.pallas_call(
        attend_kernel,
        out_shape=(
            jax.ShapeDtypeStruct((tok_rows, fw_dim), F32),
            jax.ShapeDtypeStruct((3, 8, w_cols), F32),
        ),
        in_specs=[pl.BlockSpec(memory_space=pltpu.VMEM)] * 3
        + [hbm] * 3
        + [pl.BlockSpec(memory_space=pltpu.VMEM)] * 3,
        name="window_attention",
        scratch_shapes=[pltpu.VMEM((2, WINDOW, fw_dim), BF16), pltpu.SemaphoreType.DMA((2,))],
        compiler_params=pltpu.CompilerParams(vmem_limit_bytes=VMEM_LIMIT),
        cost_estimate=pl.CostEstimate(
            flops=4 * tok_rows * (WINDOW + BLOCK) * fw_dim,
            bytes_accessed=8 * tok_rows * fw_dim,
            transcendentals=0,
        ),
    )(queries, keys, values, beside_k, before_k, prev_v, *weights)

    part_rows = w_rows // seq_count
    kept_rows = max(part_rows, SUBROWS)
    part_shape = jax.ShapeDtypeStruct((kept_rows, w_cols), BF16)
    combined, sums, *parts = pl.pallas_call(
        functools.partial(apply_kernel, steps, part_rows),
        out_shape=(
            jax.ShapeDtypeStruct((tok_rows, fw_dim), F32),
            jax.ShapeDtypeStruct((8, tok_rows), F32),
            part_shape,
            part_shape,
            part_shape,
        ),
        name="apply",
        scratch_shapes=[pltpu.VMEM((w_rows, w_cols), BF16)] * 3,
        compiler_params=pltpu.CompilerParams(vmem_limit_bytes=VMEM_LIMIT),
        cost_estimate=pl.CostEstimate(
            flops=6 * tok_rows * fw_dim * w_cols,
            bytes_accessed=12 * tok_rows * fw_dim,
            transcendentals=0,
        ),
    )(*pieces, queries, *weights, squares, attended)
    if part_rows < kept_rows:
        start = (lax.axis_index("seq") * part_rows) % kept_rows
        parts = [lax.dynamic_slice_in_dim(p, start, part_rows, 0) for p in parts]

    width = fw_dim * head_count
    if head_count == 2:
        sums = [sums, lax.ppermute(sums, "head", [(0, 1), (1, 0)])]
    else:
        sums = [lax.psum(sums, "head")]
    output = pl.pallas_call(
        functools.partial(norm_kernel, width),
        out_shape=jax.ShapeDtypeStruct((tok_rows, fw_dim), BF16),
        out_specs=hbm,
        name="norm",
        scratch_shapes=[
            pltpu.VMEM((tok_rows, fw_dim), BF16),
            pltpu.SemaphoreType.DMA((2 * tok_rows // BLOCK,)),
        ],
        compiler_params=pltpu.CompilerParams(vmem_limit_bytes=VMEM_LIMIT),
        cost_estimate=pl.CostEstimate(
            flops=4 * tok_rows * fw_dim,
            bytes_accessed=6 * tok_rows * fw_dim,
            transcendentals=0,
        ),
    )(combined, *sums, out_gain.reshape(1, fw_dim))
    return (output, *parts)


def solution(mesh):
    placed = (
        P("seq", "head"),
        P("seq", "head"),
        P("seq", "head"),
        P("seq", "head"),
        P("head", None),
        P("head", None),
        P("head", None),
        P("head"),
    )
    return jax.shard_map(
        body,
        mesh=mesh,
        in_specs=placed,
        out_specs=(
            P("seq", "head"),
            P(("head", "seq"), None),
            P(("head", "seq"), None),
            P(("head", "seq"), None),
        ),
        check_vma=False,
    )
```

```python
import functools

import jax
import jax.numpy as jnp
from jax import lax
from jax.experimental import pallas as pl
from jax.experimental.pallas import tpu as pltpu
from jax.sharding import PartitionSpec as P

ATT_DIM = 128
WINDOW = 512
BLOCK = 256
SUBROWS = 16
CHUNKS = 2


ETA_STEP = 0.5
EPSILON = 1e-06

F32 = jnp.float32
BF16 = jnp.bfloat16
VMEM_LIMIT = 40 * 1024 * 1024
VMEM_WHOLE = 62 * 1024 * 1024


def inner_rows(left_op, right_op):
    return lax.dot_general(
        left_op, right_op, (((0,), (0,)), ((), ())), preferred_element_type=F32
    )


def outer_cols(left_op, right_op):
    return lax.dot_general(
        left_op, right_op, (((1,), (1,)), ((), ())), preferred_element_type=F32
    )


def dot(left_op, right_op):
    return jnp.dot(left_op, right_op, preferred_element_type=F32)


def kernel_call(body, name, out_shape, flops, moved):
    return pl.pallas_call(
        body,
        out_shape=out_shape,
        name=name,
        compiler_params=pltpu.CompilerParams(vmem_limit_bytes=VMEM_LIMIT),
        cost_estimate=pl.CostEstimate(flops=flops, bytes_accessed=moved, transcendentals=0),
    )


def exchange_masks(peers):
    bits = [1 << at for at in range(peers.bit_length() - 1)]
    halving = [(bits[2], bits[1]), (bits[1], bits[2]), (bits[0], bits[0])]
    return halving, [(b, b) for b in bits[3:]]


def mask_here(masks):
    return jnp.where(lax.axis_index("head") % 2 == 0, masks[0], masks[1])


def bit_here(masks):
    return ((lax.axis_index("seq") & mask_here(masks)) != 0).astype(jnp.int32)


def swap(x, masks):
    peers, heads = lax.axis_size("seq"), lax.axis_size("head")
    pairs = [
        (s * heads + h, (s ^ masks[h % 2]) * heads + h)
        for s in range(peers)
        for h in range(heads)
    ]
    return lax.ppermute(x, ("seq", "head"), pairs)


def pass_odd(x):
    return lax.ppermute(x, "seq", [(i, i + 2) for i in range(1, lax.axis_size("seq") - 2, 2)])


def shift_passed(x, passed):
    peers = lax.axis_size("seq")
    odd = lax.axis_index("seq") % 2 == 1
    pairs = [(i, i + 1) for i in range(0, peers, 2)] + [(i, i - 1) for i in range(1, peers, 2)]
    return lax.ppermute(jnp.where(odd, passed, x), "seq", pairs)


def trade(x):
    peers = lax.axis_size("seq")
    return lax.ppermute(x, "seq", [(i, i ^ 1) for i in range(peers)])


def pass_on(x):
    return lax.ppermute(x, "seq", [(i, i + 2) for i in range(0, lax.axis_size("seq") - 2, 2)])


def grads_kernel(step, *refs):
    k_hbm, v_hbm, gate_hbm, up_hbm, down_hbm, rate_ref, *tail_hbms = refs[:8]
    outs = refs[8 : 8 + 2 * CHUNKS]
    refs = refs[8 + 2 * CHUNKS :]
    held, refs = refs[: 2 * CHUNKS], refs[2 * CHUNKS :]
    k_ref, v_ref, gate_ref, up_ref, down_ref, order_ref, hidden_ref, target_ref, d_gate_ref, d_up_ref = refs[:10]
    in_sems, tail_sems, out_sems = refs[10:]
    moves = ((k_hbm, k_ref), (gate_hbm, gate_ref), (up_hbm, up_ref), (v_hbm, v_ref), (down_hbm, down_ref))
    copies = [pltpu.make_async_copy(a, b, in_sems.at[at]) for at, (a, b) in enumerate(moves)]
    for copy in copies:
        copy.start()
    rows = k_ref.shape[0]
    half = held[0].shape[1]
    bit = bit_here(step)
    places = []
    for chunk in range(CHUNKS):
        for to in (1 - bit, bit):
            places.append(pl.ds(pl.multiple_of((2 * chunk + to) * half, half), half))
    tail = pl.ds(rows - WINDOW, WINDOW)
    tails = [
        pltpu.make_async_copy(ref.at[tail], tail_hbms[at], tail_sems.at[at])
        for at, ref in enumerate((k_ref, v_ref))
    ]
    copies[0].wait()
    tails[0].start()
    for at, place in enumerate(places):
        order_ref[:, place] = k_ref[:, at * half : (at + 1) * half]
    rate_col = jnp.transpose(jnp.broadcast_to(rate_ref[...], (8, rows)))[:, :1]
    for start in range(0, rows, BLOCK):
        here = slice(start, start + BLOCK)
        if start == 0:
            copies[1].wait()
        gate_pre = dot(k_ref[here], gate_ref[...])
        if start == 0:
            copies[2].wait()
        up_pre = dot(k_ref[here], up_ref[...])
        if start == 0:
            copies[3].wait()
            copies[4].wait()
            tails[1].start()
        target = (rate_col[here] * v_ref[here].astype(F32)).astype(BF16)
        target_ref[here] = target
        backward = outer_cols(target, down_ref[...])
        sigmoid_val = jax.nn.sigmoid(gate_pre)
        activated = gate_pre * sigmoid_val
        hidden = (activated * up_pre).astype(BF16)
        for at, place in enumerate(places):
            hidden_ref[here, place] = hidden[:, at * half : (at + 1) * half]
        d_up_ref[here] = (backward * activated).astype(BF16)
        derivative = sigmoid_val * (1.0 + gate_pre * (1.0 - sigmoid_val))
        d_gate_ref[here] = (backward * up_pre * derivative).astype(BF16)
    results = []
    for matrix, (left, right) in enumerate(
        ((order_ref, d_gate_ref), (order_ref, d_up_ref), (hidden_ref, target_ref))
    ):
        product = inner_rows(left[...], right[...])
        for chunk in range(CHUNKS):
            start = 2 * chunk * half
            held[chunk][matrix] = product[start : start + half].astype(BF16)
            held[CHUNKS + chunk][matrix] = product[start + half : start + 2 * half]
        for at in range(2 * CHUNKS):
            copy = pltpu.make_async_copy(held[at].at[matrix], outs[at].at[matrix], out_sems.at[matrix, at])
            copy.start()
            results.append(copy)
    for copy in tails + results:
        copy.wait()


def fold_kernel(step, *refs):
    sent_ref, next_ref = refs[-2:]
    kept_refs, came_refs = refs[: len(refs) // 2 - 1], refs[len(refs) // 2 - 1 : -2]
    half = sent_ref.shape[1] // len(kept_refs)
    bit = bit_here(step)
    for at, (kept_ref, came_ref) in enumerate(zip(kept_refs, came_refs)):
        there = slice(at * half, (at + 1) * half)
        for which, ref in ((1 - bit, sent_ref), (bit, next_ref)):
            rows = pl.ds(pl.multiple_of(which * half, half), half)
            ref[:, there] = (kept_ref[:, rows] + came_ref[:, rows].astype(F32)).astype(ref.dtype)


def fold(step, kept, came):
    rows = sum(k.shape[1] // 2 for k in kept)
    shape = (kept[0].shape[0], rows, kept[0].shape[2])
    size = shape[0] * shape[1] * shape[2]
    return kernel_call(
        functools.partial(fold_kernel, step),
        "fold",
        (jax.ShapeDtypeStruct(shape, BF16), jax.ShapeDtypeStruct(shape, F32)),
        2 * size,
        18 * size,
    )(*kept, *came)


def attend_kernel(
    q_ref, k_ref, v_ref, odd_k, even_k, prev_v, gate_ref, up_ref, down_ref, out_ref, square_ref, prev_ref, sems
):
    rows = q_ref.shape[0]
    odd = lax.axis_index("seq") % 2 == 1
    value_copy = pltpu.make_async_copy(prev_v, prev_ref.at[1], sems.at[1])
    value_copy.start()

    @pl.when(odd)
    def _():
        pltpu.make_async_copy(odd_k, prev_ref.at[0], sems.at[0]).start()

    @pl.when(jnp.logical_not(odd))
    def _():
        pltpu.make_async_copy(even_k, prev_ref.at[0], sems.at[0]).start()

    pltpu.make_async_copy(even_k, prev_ref.at[0], sems.at[0]).wait()
    value_copy.wait()
    reach = WINDOW // BLOCK
    row_at = lax.broadcasted_iota(jnp.int32, (BLOCK, BLOCK), 0)
    col_at = lax.broadcasted_iota(jnp.int32, (BLOCK, BLOCK), 1)
    first = lax.axis_index("seq") * rows
    for block in range(rows // BLOCK):
        here = slice(block * BLOCK, (block + 1) * BLOCK)
        position = first + block * BLOCK + lax.broadcasted_iota(jnp.int32, (BLOCK, 1), 0)
        counts = jnp.minimum(position + 1, WINDOW).astype(F32)
        scale = 1.0 / (counts * ATT_DIM)
        for col in range(0, q_ref.shape[1], ATT_DIM):
            cols = slice(col, col + ATT_DIM)
            query = q_ref[here, cols]
            total = None
            for other in range(block - reach, block + 1):
                if other < 0:
                    there = slice((other + reach) * BLOCK, (other + reach + 1) * BLOCK)
                    key, value = prev_ref[0, there, cols], prev_ref[1, there, cols]
                else:
                    there = slice(other * BLOCK, (other + 1) * BLOCK)
                    key, value = k_ref[there, cols], v_ref[there, cols]
                score = jnp.maximum(outer_cols(query, key), 0.0)
                weight = score * score
                if other == block:
                    weight = jnp.where(col_at <= row_at, weight, 0.0)
                if other == block - reach:
                    weight = jnp.where(col_at > row_at, weight, 0.0)
                part = dot(weight.astype(BF16), value)
                total = part if total is None else total + part
            out_ref[here, cols] = total * scale
    for at, ref in enumerate((gate_ref, up_ref, down_ref)):
        whole = jnp.square(ref[...].astype(F32))
        square_ref[at] = jnp.sum(whole.reshape(-1, 8, whole.shape[1]), axis=0)


def apply_kernel(steps, part_rows, *refs):
    count = 2 * CHUNKS
    pieces, refs = refs[:count], refs[count:]
    q_ref, gate_ref, up_ref, down_ref, square_ref, attended_ref = refs[:6]
    combined_ref, sums_ref, next_gate_ref, next_up_ref, next_down_ref = refs[6:11]
    next_refs = refs[11:]
    bits = [bit_here(m) for m in steps]
    seq_index = lax.axis_index("seq")
    blocks = [slice(start, start + BLOCK) for start in range(0, q_ref.shape[0], BLOCK)]
    ahead = []
    for at, (old_ref, new_ref) in enumerate(zip((gate_ref, up_ref, down_ref), next_refs)):
        size = old_ref.shape[0] * old_ref.shape[1]
        chunk_rows = old_ref.shape[0] // CHUNKS
        total = None
        for piece in pieces:
            part = jnp.square(piece[at].astype(F32))
            part = jnp.sum(part.reshape(-1, 8, part.shape[1]), axis=0)
            total = part if total is None else total + part
        grad_rms = jnp.sqrt(jnp.sum(total, keepdims=True) / size + EPSILON)
        weight_rms = jnp.sqrt(jnp.sum(square_ref[at], keepdims=True) / size)
        factor = ETA_STEP * weight_rms / grad_rms
        unit = chunk_rows >> len(steps)
        for chunk in range(CHUNKS):
            for arrived in range(2):
                piece = pieces[2 * chunk + arrived]
                for block in range(piece.shape[1] // unit):
                    start = chunk * chunk_rows
                    for p, bit in enumerate(bits):
                        came = arrived if p == 0 else (block >> (len(steps) - 1 - p)) & 1
                        start = start + (bit ^ came) * (chunk_rows >> (p + 1))
                    there = pl.ds(pl.multiple_of(start, unit), unit)
                    grad = piece[at, block * unit : (block + 1) * unit].astype(F32)
                    new_ref[there] = (old_ref[there].astype(F32) + factor * grad).astype(BF16)
        if at < 2:
            ahead.append([dot(q_ref[here], new_ref[...]) for here in blocks])
    for new_ref, part_ref in zip(next_refs, (next_gate_ref, next_up_ref, next_down_ref)):
        kept = part_ref.shape[0]
        start = (seq_index * part_rows) // kept * kept
        part_ref[...] = new_ref[pl.ds(pl.multiple_of(start, kept), kept)]
    ones = jnp.ones((8, attended_ref.shape[1]), BF16)
    for here, gate_pre, up_pre in zip(blocks, *ahead):
        hidden = (gate_pre * jax.nn.sigmoid(gate_pre) * up_pre).astype(BF16)
        combined = attended_ref[here] + dot(hidden, next_refs[2][...])
        combined_ref[here] = combined
        squares = combined * combined
        high = squares.astype(BF16)
        low = (squares - high.astype(F32)).astype(BF16)
        sums_ref[:, here] = outer_cols(ones, high) + outer_cols(ones, low)


def norm_kernel(width, combined_ref, *refs):
    *sums_refs, gain_ref, out_hbm, held_ref, sems = refs
    sums = sums_refs[0][...]
    for ref in sums_refs[1:]:
        sums = sums + ref[...]
    scale = jnp.transpose(lax.rsqrt(sums / width + EPSILON))[:, :1]
    copies = []
    for at, start in enumerate(range(0, held_ref.shape[0], BLOCK // 2)):
        here = slice(start, start + BLOCK // 2)
        held_ref[here] = (combined_ref[here] * scale[here] * gain_ref[...]).astype(BF16)
        copies.append(pltpu.make_async_copy(held_ref.at[here], out_hbm.at[here], sems.at[at]))
        copies[-1].start()
    for copy in copies:
        copy.wait()


def body(queries, keys, values, rates, w_gate, w_up, w_down, out_gain):
    tok_rows, fw_dim = queries.shape
    seq_count, head_count = lax.axis_size("seq"), lax.axis_size("head")
    w_rows, w_cols = w_gate.shape
    weights = (w_gate, w_up, w_down)

    chunk_rows = w_rows // CHUNKS
    steps, others = exchange_masks(seq_count)
    half = chunk_rows // 2
    hbm = pl.BlockSpec(memory_space=pltpu.HBM)
    halves = [((3, half, w_cols), kind) for kind in (BF16, F32) for _ in range(CHUNKS)]
    key_tail, value_tail, *parts = pl.pallas_call(
        functools.partial(grads_kernel, steps[0]),
        out_shape=[jax.ShapeDtypeStruct((WINDOW, fw_dim), BF16)] * 2
        + [jax.ShapeDtypeStruct(*x) for x in halves],
        in_specs=[hbm] * 5 + [pl.BlockSpec(memory_space=pltpu.VMEM)],
        out_specs=[hbm] * (2 + len(halves)),
        name="gradients",
        scratch_shapes=[pltpu.VMEM(*x) for x in halves]
        + [
            pltpu.VMEM(keys.shape, BF16),
            pltpu.VMEM(values.shape, BF16),
            pltpu.VMEM(w_gate.shape, BF16),
            pltpu.VMEM(w_up.shape, BF16),
            pltpu.VMEM(w_down.shape, BF16),
            pltpu.VMEM(keys.shape, BF16),
            pltpu.VMEM((tok_rows, w_cols), BF16),
            pltpu.VMEM(values.shape, BF16),
            pltpu.VMEM((tok_rows, w_cols), BF16),
            pltpu.VMEM((tok_rows, w_cols), BF16),
            pltpu.SemaphoreType.DMA((5,)),
            pltpu.SemaphoreType.DMA((2,)),
            pltpu.SemaphoreType.DMA((3, len(halves))),
        ],
        compiler_params=pltpu.CompilerParams(vmem_limit_bytes=VMEM_WHOLE),
        cost_estimate=pl.CostEstimate(
            flops=12 * tok_rows * fw_dim * w_cols,
            bytes_accessed=16 * tok_rows * fw_dim,
            transcendentals=0,
        ),
    )(keys, values, *weights, rates.reshape(1, tok_rows))
    sent, kept = parts[:CHUNKS], parts[CHUNKS:]
    came = [swap(x, steps[0]) for x in sent]
    beside_k = trade(key_tail)
    folded = [fold(steps[1], [k], [c]) for k, c in zip(kept, came)]
    came = [swap(x, steps[1]) for x, _ in folded]
    came[0], beside_k = lax.optimization_barrier((came[0], beside_k))
    before_k = pass_on(beside_k)
    passed = pass_odd(value_tail)
    sent, kept = fold(steps[2], [k for _, k in folded], came)
    came = swap(sent, steps[2])
    total = kept + came.astype(F32)
    for masks in others:
        total = total.astype(BF16)
        came = swap(total, masks)
        total = total.astype(F32) + came.astype(F32)
    total = total.astype(BF16)
    more = swap(total, steps[2])
    rows = total.shape[1] // CHUNKS
    pieces = []
    for c in range(CHUNKS):
        here = slice(c * rows, (c + 1) * rows)
        piece = jnp.concatenate([total[:, here], more[:, here]], axis=1)
        came = swap(piece, steps[1])
        if c == 0:
            came, passed = lax.optimization_barrier((came, passed))
            prev_v = shift_passed(value_tail, passed)
        if c == 1:
            came, before_k = lax.optimization_barrier((came, before_k))
        piece = jnp.concatenate([piece, came], axis=1)
        pieces += [piece, swap(piece, steps[0])]

    attended, squares = pl.pallas_call(
        attend_kernel,
        out_shape=(
            jax.ShapeDtypeStruct((tok_rows, fw_dim), F32),
            jax.ShapeDtypeStruct((3, 8, w_cols), F32),
        ),
        in_specs=[pl.BlockSpec(memory_space=pltpu.VMEM)] * 3
        + [hbm] * 3
        + [pl.BlockSpec(memory_space=pltpu.VMEM)] * 3,
        name="window_attention",
        scratch_shapes=[pltpu.VMEM((2, WINDOW, fw_dim), BF16), pltpu.SemaphoreType.DMA((2,))],
        compiler_params=pltpu.CompilerParams(vmem_limit_bytes=VMEM_LIMIT),
        cost_estimate=pl.CostEstimate(
            flops=4 * tok_rows * (WINDOW + BLOCK) * fw_dim,
            bytes_accessed=8 * tok_rows * fw_dim,
            transcendentals=0,
        ),
    )(queries, keys, values, beside_k, before_k, prev_v, *weights)

    part_rows = w_rows // seq_count
    kept_rows = max(part_rows, SUBROWS)
    part_shape = jax.ShapeDtypeStruct((kept_rows, w_cols), BF16)
    combined, sums, *parts = pl.pallas_call(
        functools.partial(apply_kernel, steps, part_rows),
        out_shape=(
            jax.ShapeDtypeStruct((tok_rows, fw_dim), F32),
            jax.ShapeDtypeStruct((8, tok_rows), F32),
            part_shape,
            part_shape,
            part_shape,
        ),
        name="apply",
        scratch_shapes=[pltpu.VMEM((w_rows, w_cols), BF16)] * 3,
        compiler_params=pltpu.CompilerParams(vmem_limit_bytes=VMEM_LIMIT),
        cost_estimate=pl.CostEstimate(
            flops=6 * tok_rows * fw_dim * w_cols,
            bytes_accessed=12 * tok_rows * fw_dim,
            transcendentals=0,
        ),
    )(*pieces, queries, *weights, squares, attended)
    if part_rows < kept_rows:
        start = (lax.axis_index("seq") * part_rows) % kept_rows
        parts = [lax.dynamic_slice_in_dim(p, start, part_rows, 0) for p in parts]

    width = fw_dim * head_count
    if head_count == 2:
        sums = [sums, lax.ppermute(sums, "head", [(0, 1), (1, 0)])]
    else:
        sums = [lax.psum(sums, "head")]
    output = pl.pallas_call(
        functools.partial(norm_kernel, width),
        out_shape=jax.ShapeDtypeStruct((tok_rows, fw_dim), BF16),
        out_specs=hbm,
        name="norm",
        scratch_shapes=[
            pltpu.VMEM((tok_rows, fw_dim), BF16),
            pltpu.SemaphoreType.DMA((2 * tok_rows // BLOCK,)),
        ],
        compiler_params=pltpu.CompilerParams(vmem_limit_bytes=VMEM_LIMIT),
        cost_estimate=pl.CostEstimate(
            flops=4 * tok_rows * fw_dim,
            bytes_accessed=6 * tok_rows * fw_dim,
            transcendentals=0,
        ),
    )(combined, *sums, out_gain.reshape(1, fw_dim))
    return (output, *parts)


def solution(mesh):
    placed = (
        P("seq", "head"),
        P("seq", "head"),
        P("seq", "head"),
        P("seq", "head"),
        P("head", None),
        P("head", None),
        P("head", None),
        P("head"),
    )
    return jax.shard_map(
        body,
        mesh=mesh,
        in_specs=placed,
        out_specs=(
            P("seq", "head"),
            P(("head", "seq"), None),
            P(("head", "seq"), None),
            P(("head", "seq"), None),
        ),
        check_vma=False,
    )
```
